32 devices in a mesh: dp: 8 (over z, core), fsdp: 4 (over y, x).
Axes of the slice: x: 2, y: 2, z: 4, core: 2. Of those that a mesh axis runs over, the one named last changes fastest.
Arguments:
- frames: bfloat16 [32, 512, 1024], P(('dp', 'fsdp')), may hold values from -6 to 6
- segment_ids: int32 [32, 512], P(('dp', 'fsdp')), may hold values from 0 to 2, never falling along the last dimension, each value on 1 to 256 neighbouring positions
- out_grad: bfloat16 [32, 512, 1024], P(('dp', 'fsdp')), may hold values from -6 to 6
- blocks: float32 [23, 1024, 1024], P(None, 'fsdp'), may hold values from -0.75 to 0.75
- small_params: float32 [17, 1024], replicated, may hold values from -1.5 to 1.6
- owners: int32 [23], replicated, may hold values from 0 to 7, as said below
- left_bases: float32 [24, 1024, 1024], P('dp', 'fsdp'), may hold values from -1 to 1, as said below
- right_bases: float32 [24, 1024, 1024], P('dp'), may hold values from -1 to 1, as said below
- block_first: float32 [24, 1024, 1024], P('dp', 'fsdp'), may hold values from -224 to 224
- block_second: float32 [24, 1024, 1024], P('dp', 'fsdp'), may hold values from 1638.4 to 6553.6
- small_first: float32 [17, 1024], replicated, may hold values from -384 to 384
- small_second: float32 [17, 1024], replicated, may hold values from 4096 to 16384
Outputs:
- layer_out: bfloat16 [32, 512, 1024], P(('dp', 'fsdp'))
- frames_grad: float32 [32, 512, 1024], P(('dp', 'fsdp'))
- block_grads: float32 [24, 1024, 1024], P('dp', 'fsdp')
- first_new: float32 [24, 1024, 1024], P('dp', 'fsdp')
- second_new: float32 [24, 1024, 1024], P('dp', 'fsdp')
- block_weights: float32 [24, 1024, 1024], P('dp', 'fsdp')
- small_grads: float32 [17, 1024], replicated
- small_weights: float32 [17, 1024], replicated
- small_first_new: float32 [17, 1024], replicated
- small_second_new: float32 [17, 1024], replicated
The draws below stay inside these ranges and needn't reach their ends.
Inputs may be any that keep to these rules, and one draw needn't show every extreme that they name: owners[b] is the index along dp of the group that updates block b; no index is named more than 3 times, and at least one index exactly 3 times. `left_bases`: each slot's matrix is orthogonal. `right_bases`: each slot's matrix is orthogonal.
All inputs are finite; a program needn't handle non-finite values.
Results may differ from the reference program's by a relative error of at most 0.018.
Values may be sent and summed in bfloat16 or wider, within the bound.
No kernel may reach another device: no remote copies, remote signals or barrier semaphores. Data moves between devices by JAX's collectives and lax.ppermute only.
A program may use at most 576 MiB of HBM per device.

```python
import math
import jax
import jax.numpy as jnp
import numpy as np
from jax import lax

D = 1024
HEADS = 8
FF = 4096
KERNEL = 5
LENGTH = 512
SEGS = 3
HEAD = 128
NB = 23
SMALL = 17
ROWS = 32
TOKENS = 16384
CAP = 3
SLOTS = 24
N_DP = 8


def draw_blocks(key, part):
    per_in = FF // D
    index_block = jnp.arange(NB)
    scales = jnp.full((NB,), D ** (-0.5), jnp.float32)
    outward = (index_block >= per_in) & (index_block < 2 * per_in) | (index_block >= NB - per_in)
    scales = jnp.where(outward, FF ** (-0.5), scales)
    scales = jnp.where(index_block == 2 * per_in + 3, 4.0 * D ** (-0.5), scales)
    raw_values = jax.random.truncated_normal(jax.random.fold_in(key, 3), -6.0, 6.0, (NB, D, D), jnp.float32)
    return raw_values * scales[:, None, None]


def draw_small_params(key, part):
    raw_values = jax.random.truncated_normal(jax.random.fold_in(key, 5), -3.0, 3.0, (SMALL, D), jnp.float32)
    row_index = jnp.arange(SMALL)[:, None]
    is_gain = (row_index < 5) | (row_index == 10)
    is_shift = (row_index >= 5) & (row_index < 10) | (row_index == 11)
    return jnp.where(is_gain, 1.0 + 0.2 * raw_values, jnp.where(is_shift, 0.3 * raw_values, 0.5 * raw_values))


def draw_owners(key, part):
    slot_total = CAP * N_DP
    key_full, key_rest, key_order = jax.random.split(jax.random.fold_in(key, 7), 3)
    full_owner = jax.random.randint(key_full, (), 0, N_DP)
    others = (full_owner * CAP + CAP + jnp.arange(slot_total - CAP)) % slot_total
    others = jax.random.permutation(key_rest, others)[:NB - CAP]
    chosen = jnp.concatenate([full_owner * CAP + jnp.arange(CAP), others])
    chosen = jax.random.permutation(key_order, chosen)
    return (chosen // CAP).astype(jnp.int32)


def slot_orders(key):
    return jax.vmap(lambda single: jax.random.permutation(single, D))(jax.random.split(key, SLOTS)).astype(jnp.int32)


def signed_hadamard(key):
    key_perm, key_row, key_col = jax.random.split(key, 3)
    orders = slot_orders(key_perm)
    row_sign = (2 * jax.random.randint(key_row, (SLOTS, D, 1), 0, 2) - 1).astype(jnp.float32)
    col_sign = (2 * jax.random.randint(key_col, (SLOTS, 1, D), 0, 2) - 1).astype(jnp.float32)
    row_index = jnp.arange(D, dtype=jnp.int32)[None, :, None]
    common = row_index & orders[:, None, :]
    parity = jnp.zeros(common.shape, jnp.int32)
    for bit_number in range(D.bit_length()):
        parity = parity + (common >> bit_number & 1)
    parity = parity & 1
    return (1.0 - 2.0 * parity.astype(jnp.float32)) * row_sign * col_sign * D ** (-0.5)


def turn_columns(matrix, key):
    paired = matrix.reshape(SLOTS, D, D // 2, 2)
    angles = jax.random.uniform(key, (SLOTS, 1, D // 2), jnp.float32, -math.pi, math.pi)
    cosine = jnp.cos(angles)
    sine = jnp.sin(angles)
    first_col = paired[..., 0]
    second_col = paired[..., 1]
    turned = jnp.stack([cosine * first_col + sine * second_col, cosine * second_col - sine * first_col], axis=-1)
    return turned.reshape(SLOTS, D, D)


def turn_rows(matrix, key):
    paired = matrix.reshape(SLOTS, D // 2, 2, D)
    angles = jax.random.uniform(key, (SLOTS, D // 2, 1), jnp.float32, -math.pi, math.pi)
    cosine = jnp.cos(angles)
    sine = jnp.sin(angles)
    first_row = paired[:, :, 0]
    second_row = paired[:, :, 1]
    turned = jnp.stack([cosine * first_row + sine * second_row, cosine * second_row - sine * first_row], axis=2)
    return turned.reshape(SLOTS, D, D)


def orthogonal_bases(key):
    base = signed_hadamard(jax.random.fold_in(key, 1))
    base = turn_columns(base, jax.random.fold_in(key, 2))
    base = turn_rows(base, jax.random.fold_in(key, 3))
    return base


def draw_left_bases(key, part):
    return orthogonal_bases(jax.random.fold_in(key, 11))


def draw_right_bases(key, part):
    return orthogonal_bases(jax.random.fold_in(key, 13))


def level_of(own_key, extent, cuts, least, high):
    def one(axis_at, shards_of):
        steps = jax.random.uniform(jax.random.fold_in(jax.random.fold_in(own_key, 6), axis_at), (shards_of,), jnp.float32, least / len(cuts), high / len(cuts))
        return jnp.repeat(jnp.exp(steps), extent[axis_at] // shards_of).reshape((-1,) + (1,) * (len(extent) - axis_at - 1))

    factor_of = one(*cuts[0])
    for cut in cuts[1:]:
        factor_of = factor_of * one(*cut)
    return factor_of


def profile(number_of, total, limit, skew):
    loads = [(1 << 20) // math.isqrt(rank ** skew) + 1 for rank in range(2, number_of + 1)]
    surplus, counts = total - limit - (number_of - 1), [1] * (number_of - 1)
    while surplus > 0:
        candidates = [i for i in range(number_of - 1) if counts[i] < limit]
        pool, left = sum([loads[i] for i in candidates]), surplus
        for i in candidates:
            more = min(limit - counts[i], max(1, left * loads[i] // pool), surplus)
            counts[i] = counts[i] + more
            surplus = surplus - more
    return np.array([limit] + counts)


def ragged(rng, count, total, bound, lean):
    if count == 2:
        one = jax.random.randint(rng, (), max(1, total - bound), min(bound, total - 1) + 1)
        return jnp.stack([one, total - one])
    lengths = jnp.asarray(profile(count, total, bound, lean), jnp.int32)
    twos = (count - 1) // 2
    giver, sink = lengths[1:1 + 2 * twos:2], lengths[2:2 + 2 * twos:2]
    slack = jnp.minimum(giver - 1, bound - sink)
    shifted = jax.random.randint(jax.random.fold_in(rng, 1), (twos,), 0, 1 << 20) % (slack + 1)
    lengths = lengths.at[1:1 + 2 * twos:2].set(giver - shifted).at[2:2 + 2 * twos:2].set(sink + shifted)
    return lengths[jax.random.permutation(jax.random.fold_in(rng, 2), count)]


def bell_draw(stream_key, extent, deviation, reach, cuts=(), kind=jnp.bfloat16):
    loudness = level_of(stream_key, extent, cuts, -0.22, 0.18) if cuts else 1.0
    drawn = jax.random.normal(stream_key, extent, jnp.float32) * deviation * loudness
    return jnp.minimum(jnp.maximum(drawn, -reach), reach).astype(kind)


def setup_inputs(seed: int = 0) -> dict:
    splits = jax.random.split(jax.random.key(seed), 13)
    return {
        "frames": bell_draw(splits[0], (ROWS, LENGTH, D), 1.0, 6.0, ((0, 32),)),
        "segment_ids": jax.vmap(lambda own: jnp.searchsorted(jnp.cumsum(ragged(own, SEGS, LENGTH, LENGTH // 2, 0)), jnp.arange(LENGTH), side="right"))(jax.random.split(splits[1], ROWS)).reshape((ROWS, LENGTH)).astype(jnp.int32),
        "out_grad": bell_draw(splits[2], (ROWS, LENGTH, D), 1.0, 6.0, ((0, 32),)),
        "blocks": draw_blocks(jax.random.fold_in(splits[12], 71), 0),
        "small_params": draw_small_params(jax.random.fold_in(splits[12], 71), 0),
        "owners": draw_owners(jax.random.fold_in(splits[12], 71), 0),
        "left_bases": draw_left_bases(jax.random.fold_in(splits[12], 71), 0),
        "right_bases": draw_right_bases(jax.random.fold_in(splits[12], 71), 0),
        "block_first": bell_draw(splits[8], (SLOTS, D, D), (0.3 * TOKENS ** 0.5), 224.0, ((0, 8), (1, 4)), jnp.float32),
        "block_second": jnp.clip(jnp.exp(math.log(6553.6) - 1.3862944 * jax.random.uniform(splits[9], (SLOTS, D, D), jnp.float32) ** level_of(splits[9], (SLOTS, D, D), ((0, 8), (1, 4)), -0.2, 0.2)), 1638.4, 6553.6),
        "small_first": bell_draw(splits[10], (SMALL, D), (0.5 * TOKENS ** 0.5), 384.0, (), jnp.float32),
        "small_second": jnp.clip(jnp.exp(jax.random.uniform(splits[11], (SMALL, D), jnp.float32, math.log(4096.0), math.log(16384.0))), 4096.0, 16384.0),
    }


@jax.custom_vjp
def low(v):
    return lax.optimization_barrier(v.astype(jnp.bfloat16)).astype(jnp.float32)

@jax.custom_vjp
def low_back(v):
    return v

def low_keep(v):
    return (low(v), None)

def low_pass(kept, grad):
    return (grad,)

def back_keep(v):
    return (v, None)

def back_low(kept, grad):
    return (low(grad),)
low.defvjp(low_keep, low_pass)
low_back.defvjp(back_keep, back_low)
EPS_NORM = 1e-05
EPS_ADAM = 1e-08
LEARN_RATE = 0.02
SMALL_RATE = 0.3
DECAY_WEIGHT = 0.01
BETA_DECAY = 0.5
MASKED = -1000000000.0
HIGHEST = lax.Precision.HIGHEST

def norm_apply(values, scale_row, shift_row):
    average = lax.optimization_barrier(jnp.mean(values, axis=-1, keepdims=True))
    centered = values - average
    variance = lax.optimization_barrier(jnp.mean(centered * centered, axis=-1, keepdims=True))
    return centered * lax.rsqrt(variance + EPS_NORM) * scale_row + shift_row

def swish(values):
    return values * jax.nn.sigmoid(values)

def depthwise(gated_rows, kernel_taps, segment_ids):
    length = gated_rows.shape[1]
    margin = KERNEL // 2
    padded = jnp.pad(gated_rows, ((0, 0), (margin, margin), (0, 0)))
    segment_pad = jnp.pad(segment_ids, ((0, 0), (margin, margin)), constant_values=-1)
    summed = jnp.zeros_like(gated_rows)
    for offset in range(KERNEL):
        matched = (segment_pad[:, offset:offset + length] == segment_ids)[:, :, None]
        summed = summed + kernel_taps[offset] * jnp.where(matched, padded[:, offset:offset + length], 0.0)
    return summed

def slot_tables(owners, groups, count_blocks):
    capacity = (count_blocks + groups - 1) // groups
    block_index = jnp.arange(count_blocks, dtype=jnp.int32)
    earlier = (owners[None, :] == owners[:, None]) & (block_index[None, :] < block_index[:, None])
    ranking = lax.optimization_barrier(jnp.sum(earlier.astype(jnp.int32), axis=1)).astype(jnp.int32)
    slot_of = (owners * capacity + ranking).astype(jnp.int32)
    matches = slot_of[None, :] == jnp.arange(capacity * groups, dtype=jnp.int32)[:, None]
    slot_used = lax.optimization_barrier(jnp.sum(matches.astype(jnp.int32), axis=1)).astype(jnp.int32)
    slot_block = lax.optimization_barrier(jnp.sum(jnp.where(matches, block_index[None, :], 0), axis=1)).astype(jnp.int32)
    return (slot_block, slot_used)

def attend_row(arrays):
    queries, keys_row, values_row, segment_row = arrays
    scores = low_back(jnp.einsum('qhe,khe->hqk', queries, keys_row, precision=HIGHEST))
    matched = (segment_row[:, None] == segment_row[None, :])[None]
    scores = jnp.where(matched, scores, MASKED)
    highest = lax.optimization_barrier(jnp.max(scores, axis=-1, keepdims=True))
    exponent = jnp.exp(scores - highest)
    attention = low(exponent / lax.optimization_barrier(jnp.sum(exponent, axis=-1, keepdims=True)))
    return jnp.einsum('hqk,khe->qhe', attention, values_row, precision=HIGHEST)

def feed_forward(hidden, scale_row, shift_row, weight_in, weight_out):
    normed = low(norm_apply(hidden, scale_row, shift_row))
    lifted = low_back(jnp.einsum('td,jdh->tjh', normed, weight_in, precision=HIGHEST))
    activated = low(swish(lifted))
    result = low_back(jnp.einsum('tjh,jhe->te', activated, weight_out, precision=HIGHEST))
    return hidden + 0.5 * result

def layer_forward(frames32, blocks32, small32, segment_ids):
    rows_all = frames32.shape[0]
    per_in = FF // D
    base_attn = 2 * per_in
    base_last = base_attn + 7
    weights = low(blocks32)
    gains = small32[0:5]
    shifts = small32[5:10]
    kernel_taps = small32[12:12 + KERNEL]
    hidden = frames32.reshape(rows_all * LENGTH, D)
    hidden = feed_forward(hidden, gains[0], shifts[0], weights[0:per_in], weights[per_in:base_attn])
    normed = low(norm_apply(hidden, gains[1], shifts[1]))
    projected = low_back(jnp.einsum('td,jdh->tjh', normed, weights[base_attn:base_attn + 3], precision=HIGHEST))
    split_shape = (rows_all, LENGTH, HEADS, HEAD)
    queries = low(projected[:, 0] * HEAD ** (-0.5)).reshape(split_shape)
    keys_all = low(projected[:, 1]).reshape(split_shape)
    values_all = low(projected[:, 2]).reshape(split_shape)
    context = lax.map(jax.checkpoint(attend_row), (queries, keys_all, values_all, segment_ids))
    context = low(low_back(context.reshape(rows_all * LENGTH, D)))
    hidden = hidden + low_back(jnp.dot(context, weights[base_attn + 3], precision=HIGHEST))
    normed = low(norm_apply(hidden, gains[2], shifts[2]))
    before = low_back(jnp.einsum('td,jdh->tjh', normed, weights[base_attn + 4:base_attn + 6], precision=HIGHEST))
    gated_rows = before[:, 0] * jax.nn.sigmoid(before[:, 1])
    convolved = depthwise(gated_rows.reshape(rows_all, LENGTH, D), kernel_taps, segment_ids).reshape(rows_all * LENGTH, D)
    average = lax.optimization_barrier(jnp.mean(convolved, axis=0))
    variance = lax.optimization_barrier(jnp.mean(convolved * convolved, axis=0)) - average * average
    batch_normed = (convolved - average) * lax.rsqrt(variance + EPS_NORM) * small32[10] + small32[11]
    activated = low(swish(batch_normed))
    hidden = hidden + low_back(jnp.dot(activated, weights[base_attn + 6], precision=HIGHEST))
    hidden = feed_forward(hidden, gains[3], shifts[3], weights[base_last:base_last + per_in], weights[base_last + per_in:base_last + 2 * per_in])
    return norm_apply(hidden, gains[4], shifts[4]).reshape(rows_all, LENGTH, D)

def update_slot(arrays):
    gradient, left_basis, right_basis, first_old, second_old, master = arrays
    rotated = jnp.dot(jnp.dot(left_basis.T, gradient, precision=HIGHEST), right_basis, precision=HIGHEST)
    first_step = BETA_DECAY * first_old + (1.0 - BETA_DECAY) * rotated
    second_step = BETA_DECAY * second_old + (1.0 - BETA_DECAY) * rotated * rotated
    direction = first_step / (jnp.sqrt(second_step) + EPS_ADAM)
    update = jnp.dot(jnp.dot(left_basis, direction, precision=HIGHEST), right_basis.T, precision=HIGHEST)
    return (first_step, second_step, master - LEARN_RATE * (update + DECAY_WEIGHT * master))

def reference(frames, segment_ids, out_grad, blocks, small_params, owners, left_bases, right_bases, block_first, block_second, small_first, small_second):

    def forward_only(frames32, blocks32, small32):
        return layer_forward(frames32, blocks32, small32, segment_ids)
    layer_value, pullback = jax.vjp(forward_only, frames.astype(jnp.float32), blocks, small_params)
    frames_grad, blocks_grad, small_grads = pullback(out_grad.astype(jnp.float32))
    slot_block, slot_used = slot_tables(owners, N_DP, NB)
    used_float = slot_used.astype(jnp.float32)[:, None, None]
    slot_grads = blocks_grad[slot_block] * used_float
    slot_masters = blocks[slot_block]
    first_new, second_new, weights_new = lax.map(update_slot, (slot_grads, left_bases, right_bases, block_first, block_second, slot_masters))
    small_first_new = BETA_DECAY * small_first + (1.0 - BETA_DECAY) * small_grads
    small_second_new = BETA_DECAY * small_second + (1.0 - BETA_DECAY) * small_grads * small_grads
    small_weights = small_params - SMALL_RATE * small_first_new / (jnp.sqrt(small_second_new) + EPS_ADAM)
    return (layer_value.astype(jnp.bfloat16), frames_grad, slot_grads, first_new * used_float, second_new * used_float, weights_new * used_float, small_grads, small_weights, small_first_new, small_second_new)
```

```python
import jax
import jax.numpy as jnp
from jax import lax
from jax.sharding import PartitionSpec as P

D = 1024
HEADS = 8
FF = 4096
KERNEL = 5
LENGTH = 512
HEAD = 128

EPS_NORM = 1e-05
EPS_ADAM = 1e-08
LEARN_RATE = 0.02
SMALL_RATE = 0.3
DECAY_WEIGHT = 0.01
BETA_DECAY = 0.5
MASKED = -1000000000.0
AXES = ("dp", "fsdp")
BF = jnp.bfloat16
F32 = jnp.float32


def bits_of(size):
    return [1 << k for k in range(size.bit_length() - 1)]


def swap(value, dp_mask, fsdp_mask):
    n_dp, n_fsdp = lax.axis_size("dp"), lax.axis_size("fsdp")
    pairs = [
        (d * n_fsdp + f, (d ^ dp_mask) * n_fsdp + (f ^ fsdp_mask))
        for d in range(n_dp)
        for f in range(n_fsdp)
    ]
    return lax.ppermute(value, AXES, pairs)


def total(value):
    for mask in bits_of(lax.axis_size("fsdp")):
        value = value + swap(value, 0, mask)
    for mask in bits_of(lax.axis_size("dp")):
        value = value + swap(value, mask, 0)
    return value


def after(value, *earlier):
    return lax.optimization_barrier((value, *earlier))[0]


def pick(value, axis, index):
    return lax.dynamic_index_in_dim(value, index, axis, keepdims=False)


def place(value, shape, starts):
    return value, shape, starts


def norm_apply(values, scale_row, shift_row):
    average = jnp.mean(values, axis=-1, keepdims=True)
    centered = values - average
    variance = jnp.mean(centered * centered, axis=-1, keepdims=True)
    return centered * lax.rsqrt(variance + EPS_NORM) * scale_row + shift_row


def swish(values):
    return values * jax.nn.sigmoid(values)


def depthwise(gated_rows, kernel_taps, segment_ids):
    length = gated_rows.shape[1]
    margin = KERNEL // 2
    padded = jnp.pad(gated_rows, ((0, 0), (margin, margin), (0, 0)))
    segment_pad = jnp.pad(segment_ids, ((0, 0), (margin, margin)), constant_values=-1)
    summed = jnp.zeros_like(gated_rows)
    for offset in range(KERNEL):
        matched = (segment_pad[:, offset : offset + length] == segment_ids)[:, :, None]
        summed = summed + kernel_taps[offset] * jnp.where(
            matched, padded[:, offset : offset + length], 0.0
        )
    return summed


def slot_tables(owners, groups, count_blocks):
    capacity = (count_blocks + groups - 1) // groups
    block_index = jnp.arange(count_blocks, dtype=jnp.int32)
    earlier = (owners[None, :] == owners[:, None]) & (block_index[None, :] < block_index[:, None])
    ranking = jnp.sum(earlier.astype(jnp.int32), axis=1)
    slot_of = owners * capacity + ranking
    return slot_of[None, :] == jnp.arange(capacity * groups, dtype=jnp.int32)[:, None]


def gated_conv(pre_a, pre_g, kernel_taps, segment_ids):
    rows_here = segment_ids.shape[0]
    gated_rows = pre_a * jax.nn.sigmoid(pre_g)
    shaped = gated_rows.reshape(rows_here, -1, gated_rows.shape[-1])
    return depthwise(shaped, kernel_taps, segment_ids).reshape(gated_rows.shape)


def masked_scores(queries, keys_row, segment_row):
    scores = jnp.einsum("qhe,khe->hqk", queries, keys_row, preferred_element_type=F32)
    matched = (segment_row[:, None] == segment_row[None, :])[None]
    return jnp.where(matched, scores, MASKED)


def attend_forward(arrays):
    queries, keys_row, values_row, segment_row = arrays
    scores = masked_scores(queries, keys_row, segment_row)
    highest = jnp.max(scores, axis=-1, keepdims=True)
    exponent = jnp.exp(scores - highest)
    summed = jnp.sum(exponent, axis=-1, keepdims=True)
    attention = (exponent / summed).astype(BF)
    context = jnp.einsum("hqk,khe->qhe", attention, values_row, preferred_element_type=F32)
    return (context, (highest + jnp.log(summed))[..., 0])


def attend_backward(arrays):
    queries, keys_row, values_row, segment_row, log_total, context_grad = arrays
    scores = masked_scores(queries, keys_row, segment_row)
    attention = jnp.exp(scores - log_total[..., None])
    attention_grad = jnp.einsum(
        "qhe,khe->hqk", context_grad, values_row, preferred_element_type=F32
    )
    score_grad = attention * (
        attention_grad - jnp.sum(attention_grad * attention, axis=-1, keepdims=True)
    )
    score_low = score_grad.astype(BF)
    query_grad = jnp.einsum("hqk,khe->qhe", score_low, keys_row, preferred_element_type=F32)
    key_grad = jnp.einsum("hqk,qhe->khe", score_low, queries, preferred_element_type=F32)
    value_grad = jnp.einsum(
        "hqk,qhe->khe", attention.astype(BF), context_grad, preferred_element_type=F32
    )
    return (query_grad, key_grad, value_grad)


def mm(left, right):
    return jnp.dot(left, right, preferred_element_type=F32)


def mm_t(left, right):
    return lax.dot_general(left, right, (((1,), (1,)), ((), ())), preferred_element_type=F32)


def t_mm(left, right):
    return lax.dot_general(left, right, (((0,), (0,)), ((), ())), preferred_element_type=F32)


class Gather:
    def __init__(self, blocks):
        self.blocks = blocks
        self.n_fsdp = lax.axis_size("fsdp")
        self.core = lax.axis_index("dp") % 2
        self.mine = lax.axis_index("fsdp")
        self.half = blocks.shape[1] // 2
        self.recent = []

    def chunk(self, low, high):
        count = high - low
        piece = self.blocks[low:high].reshape(count, 2, self.half, D).astype(BF)
        own = pick(piece, 1, self.core)
        if len(self.recent) >= 2:
            own = after(own, self.recent[-2])
        masks = bits_of(self.n_fsdp)
        if len(self.recent) % 2:
            masks = masks[::-1]
        pieces = {0: own}
        for mask in masks:
            for known, held in list(pieces.items()):
                pieces[known | mask] = swap(held, 0, mask)
            if mask == masks[0]:
                self.recent.append(pieces[mask])
        other = {0: pick(piece, 1, 1 - self.core)}
        for known, held in pieces.items():
            if known:
                other[known] = swap(held, 1, 0)
        full = jnp.zeros((count, self.n_fsdp, 2, self.half, D), BF)
        for known in pieces:
            at = self.mine ^ known
            for held, side in ((pieces[known], self.core), (other[known], 1 - self.core)):
                full = lax.dynamic_update_slice(full, held[:, None, None], (0, at, side, 0, 0))
        return full.reshape(count, D, D)


class Reduce:
    def __init__(self, rows_own):
        self.n_fsdp = lax.axis_size("fsdp")
        self.n_dp = lax.axis_size("dp")
        self.core = lax.axis_index("dp") % 2
        self.dp = lax.axis_index("dp")
        self.mine = lax.axis_index("fsdp")
        self.half = rows_own // 2
        self.count = 0

    def group(self, left, right):
        tokens = left.shape[0]
        wide = left.shape[1] // D
        tall = right.shape[1] // D
        split = left.reshape(tokens, wide, self.n_fsdp, 2, self.half)
        sides = []
        for side in (1 - self.core, self.core):
            sides.append(pick(split, 3, side).reshape(tokens, -1))
        away = t_mm(sides[0], right).astype(BF)
        arrived = swap(away, 1, 0)
        held = (t_mm(sides[1], right) + arrived.astype(F32)).astype(BF)
        held = held.reshape(wide, self.n_fsdp, self.half, tall, D)
        masks = bits_of(self.n_fsdp)
        order = masks[::-1] if self.count % 2 else masks
        self.count += 1
        left_masks = list(masks)
        for mask in order:
            place_at = left_masks.index(mask)
            below = 1 << place_at
            shape = held.shape
            parted = held.reshape(shape[0], shape[1] // (2 * below), 2, below, *shape[2:])
            bit = (self.mine // mask) % 2
            arrived = swap(pick(parted, 2, 1 - bit), 0, mask)
            kept = pick(parted, 2, bit)
            held = (kept.astype(F32) + arrived.astype(F32)).astype(BF)
            held = held.reshape(shape[0], shape[1] // 2, *shape[2:])
            left_masks.remove(mask)
        held = held.reshape(wide, self.half, tall, D)
        for mask in bits_of(self.n_dp)[1:]:
            shape = held.shape
            parted = held.reshape(shape[0], 2, shape[1] // 2, *shape[2:])
            bit = (self.dp // mask) % 2
            arrived = swap(pick(parted, 1, 1 - bit), mask, 0)
            held = (pick(parted, 1, bit).astype(F32) + arrived.astype(F32)).astype(BF)
        if tall > 1:
            return jnp.moveaxis(held[0], 1, 0)
        return held[:, :, 0]


def feed_forward(hidden, scale_row, shift_row, weights_in, weights_out):
    normed, norm_pullback = jax.vjp(norm_apply, hidden, scale_row, shift_row)
    normed_low = normed.astype(BF)
    lifted, acted = [], []
    for part in weights_in:
        up = jnp.einsum("td,jdh->tjh", normed_low, part, preferred_element_type=F32)
        up = up.reshape(up.shape[0], -1)
        lifted.append(up.astype(BF))
        acted.append(swish(up).astype(BF))
    result = sum(mm(s, part.reshape(-1, D)) for s, part in zip(acted, weights_out))
    return hidden + 0.5 * result, (norm_pullback, normed_low, lifted, acted)


def feed_backward(gradient, saved, weights_in, weights_out, reduce):
    norm_pullback, normed_low, lifted, acted = saved
    result_low = (0.5 * gradient).astype(BF)
    out_grads, in_grads, normed_grad = [], [], 0.0
    for up, s, part_in, part_out in zip(lifted, acted, weights_in, weights_out):
        out_grads.append(reduce.group(s, result_low))
        acted_grad = mm_t(result_low, part_out.reshape(-1, D))
        up = up.astype(F32)
        gate = jax.nn.sigmoid(up)
        low = (acted_grad * (gate * (1.0 + up * (1.0 - gate)))).astype(BF)
        in_grads.append(reduce.group(normed_low, low))
        low = low.reshape(low.shape[0], -1, D)
        normed_grad = normed_grad + jnp.einsum(
            "tjh,jdh->td", low, part_in, preferred_element_type=F32
        )
    hidden_grad, scale_grad, shift_grad = norm_pullback(normed_grad)
    return gradient + hidden_grad, scale_grad, shift_grad, in_grads, out_grads


def per_device(
    frames,
    segment_ids,
    out_grad,
    blocks,
    small_params,
    owners,
    left_bases,
    right_bases,
    block_first,
    block_second,
    small_first,
    small_second,
):
    rows_here = frames.shape[0]
    tokens = rows_here * LENGTH
    n_blocks = blocks.shape[0]
    rows_own = blocks.shape[1]
    scale_head = HEAD ** (-0.5)
    n_dp = lax.axis_size("dp")
    n_fsdp = lax.axis_size("fsdp")
    mine = lax.axis_index("fsdp")
    count_all = tokens * n_dp * n_fsdp
    gather = Gather(blocks)
    reduce = Reduce(rows_own)
    w_in1 = [gather.chunk(0, 2), gather.chunk(2, 4)]
    w_out1 = [gather.chunk(4, 6), gather.chunk(6, 8)]
    w_qk = gather.chunk(8, 10)
    w_vo = gather.chunk(10, 12)
    w_point = gather.chunk(12, 14)
    w_back = gather.chunk(14, 15)[0]
    w_in2 = [gather.chunk(15, 17), gather.chunk(17, 19)]
    w_out2 = [gather.chunk(19, 21), gather.chunk(21, 23)]
    gains = small_params[0:5]
    shifts = small_params[5:10]
    bn_gain = small_params[10]
    bn_shift = small_params[11]
    kernel_taps = small_params[12 : 12 + KERNEL]

    start_x = frames.astype(F32).reshape(tokens, D)
    first_x, first_saved = feed_forward(start_x, gains[0], shifts[0], w_in1, w_out1)
    normed, attn_pullback = jax.vjp(norm_apply, first_x, gains[1], shifts[1])
    attn_low = normed.astype(BF)
    split_shape = (rows_here, LENGTH, HEADS, HEAD)
    queries = (mm(attn_low, w_qk[0]) * scale_head).astype(BF).reshape(split_shape)
    keys_all = mm(attn_low, w_qk[1]).astype(BF).reshape(split_shape)
    values_all = mm(attn_low, w_vo[0]).astype(BF).reshape(split_shape)
    context, log_total = lax.map(attend_forward, (queries, keys_all, values_all, segment_ids))
    context_low = context.reshape(tokens, D).astype(BF)
    second_x = first_x + mm(context_low, w_vo[1])
    normed, conv_pullback = jax.vjp(norm_apply, second_x, gains[2], shifts[2])
    conv_low = normed.astype(BF)
    convolved, gated_pullback = jax.vjp(
        lambda pre_a, pre_g, taps_in: gated_conv(pre_a, pre_g, taps_in, segment_ids),
        mm(conv_low, w_point[0]),
        mm(conv_low, w_point[1]),
        kernel_taps,
    )
    stats = total(
        jnp.stack([jnp.sum(convolved, axis=0), jnp.sum(convolved * convolved, axis=0)])
    )
    average = stats[0] / count_all
    inverse_dev = lax.rsqrt(stats[1] / count_all - average * average + EPS_NORM)
    standard = (convolved - average) * inverse_dev
    activated, bn_swish_pullback = jax.vjp(swish, standard * bn_gain + bn_shift)
    activated_low = activated.astype(BF)
    third_x = second_x + mm(activated_low, w_back)
    fourth_x, last_saved = feed_forward(third_x, gains[3], shifts[3], w_in2, w_out2)
    layer_value, final_pullback = jax.vjp(norm_apply, fourth_x, gains[4], shifts[4])
    layer_out = layer_value.astype(BF).reshape(rows_here, LENGTH, D)

    grad_x, final_gain, final_shift = final_pullback(out_grad.astype(F32).reshape(tokens, D))
    grad_x, ffn2_gain, ffn2_shift, grad_in2, grad_out2 = feed_backward(
        grad_x, last_saved, w_in2, w_out2, reduce
    )
    branch_low = grad_x.astype(BF)
    grad_back = reduce.group(activated_low, branch_low)
    (bn_grad,) = bn_swish_pullback(mm_t(branch_low, w_back))
    sums = total(jnp.stack([jnp.sum(bn_grad, axis=0), jnp.sum(bn_grad * standard, axis=0)]))
    shift_sum, gain_sum = sums[0], sums[1]
    conv_grad = (
        bn_gain
        * inverse_dev
        * (bn_grad - shift_sum / count_all - standard * (gain_sum / count_all))
    )
    grad_a, grad_g, taps_grad = gated_pullback(conv_grad)
    grad_a, grad_g = grad_a.astype(BF), grad_g.astype(BF)
    grad_point = reduce.group(conv_low, jnp.concatenate([grad_a, grad_g], axis=1))
    part_x, conv_gain, conv_shift = conv_pullback(
        mm_t(grad_a, w_point[0]) + mm_t(grad_g, w_point[1])
    )
    grad_x = grad_x + part_x
    branch_low = grad_x.astype(BF)
    grad_proj = reduce.group(context_low, branch_low)
    context_grad = mm_t(branch_low, w_vo[1]).astype(BF).reshape(split_shape)
    query_grad, key_grad, value_grad = lax.map(
        attend_backward, (queries, keys_all, values_all, segment_ids, log_total, context_grad)
    )
    query_low = (query_grad.reshape(tokens, D) * scale_head).astype(BF)
    key_low = key_grad.reshape(tokens, D).astype(BF)
    value_low = value_grad.reshape(tokens, D).astype(BF)
    grad_attn = reduce.group(attn_low, jnp.concatenate([query_low, key_low, value_low], axis=1))
    part_x, attn_gain, attn_shift = attn_pullback(
        mm_t(query_low, w_qk[0]) + mm_t(key_low, w_qk[1]) + mm_t(value_low, w_vo[0])
    )
    grad_x = grad_x + part_x
    grad_x, ffn1_gain, ffn1_shift, grad_in1, grad_out1 = feed_backward(
        grad_x, first_saved, w_in1, w_out1, reduce
    )
    frames_grad = grad_x.reshape(rows_here, LENGTH, D)
    local_small = jnp.concatenate(
        [
            jnp.stack([ffn1_gain, attn_gain, conv_gain, ffn2_gain, final_gain]),
            jnp.stack([ffn1_shift, attn_shift, conv_shift, ffn2_shift, final_shift]),
            taps_grad,
        ],
        axis=0,
    )
    summed_small = total(local_small)
    small_grads = jnp.concatenate(
        [summed_small[0:10], gain_sum[None], shift_sum[None], summed_small[10:]], axis=0
    )

    parts = jnp.concatenate(
        [
            *grad_in1,
            *grad_out1,
            grad_attn,
            grad_proj,
            grad_point,
            grad_back,
            *grad_in2,
            *grad_out2,
        ],
        axis=0,
    )
    capacity = (n_blocks + n_dp - 1) // n_dp
    matches = slot_tables(owners, n_dp, n_blocks)
    piece = parts.shape[1]
    sent = mm(matches.astype(BF), parts.reshape(n_blocks, -1)).astype(BF)
    sent = sent.reshape(n_dp, capacity * piece, D)
    came = lax.all_to_all(sent, "dp", 0, 0, tiled=False)
    n_bits = n_dp.bit_length() - 1
    came = came.reshape(*([2] * n_bits), capacity, piece, D)
    came = came.transpose(n_bits, *range(n_bits - 1, -1, -1), n_bits + 1, n_bits + 2)
    owned_low = came.reshape(capacity, rows_own, D)
    owned = owned_low.astype(F32)

    dp_here = lax.axis_index("dp")
    my_match = lax.dynamic_slice_in_dim(
        matches.astype(jnp.int32), dp_here * capacity, capacity, axis=0
    )
    my_blocks = jnp.sum(my_match * jnp.arange(n_blocks, dtype=jnp.int32)[None], axis=1)
    my_used = jnp.sum(my_match, axis=1).astype(F32)
    first_list, second_list, weight_list = [], [], []
    masks = bits_of(n_fsdp)
    for slot in range(capacity):
        left_rows = left_bases[slot].astype(BF)
        right_basis = right_bases[slot].astype(BF)
        product = mm(owned_low[slot], right_basis).astype(BF)
        spread = t_mm(left_rows, product).astype(BF).reshape(n_fsdp, rows_own, D)
        halves = []
        for side, order in ((0, masks), (1, masks[::-1])):
            held = spread[:, :, side * (D // 2) : (side + 1) * (D // 2)]
            left_masks = list(masks)
            for mask in order:
                below = 1 << left_masks.index(mask)
                shape = held.shape
                parted = held.reshape(shape[0] // (2 * below), 2, below, *shape[1:])
                bit = (mine // mask) % 2
                arrived = swap(pick(parted, 1, 1 - bit), 0, mask)
                held = pick(parted, 1, bit).astype(F32) + arrived.astype(F32)
                held = held.reshape(shape[0] // 2, *shape[1:])
                left_masks.remove(mask)
                if left_masks:
                    held = held.astype(BF)
            halves.append(held[0])
        rotated = jnp.concatenate(halves, axis=1)
        first_step = BETA_DECAY * block_first[slot] + (1.0 - BETA_DECAY) * rotated
        second_step = BETA_DECAY * block_second[slot] + (1.0 - BETA_DECAY) * rotated * rotated
        direction = (first_step / (jnp.sqrt(second_step) + EPS_ADAM)).astype(BF)
        mixed = []
        left_split = left_rows.reshape(rows_own, n_fsdp, rows_own)
        for side, order in ((0, masks), (1, masks[::-1])):
            pieces = {0: direction[:, side * (D // 2) : (side + 1) * (D // 2)]}
            for mask in order:
                for known, held in list(pieces.items()):
                    pieces[known | mask] = swap(held, 0, mask)
            mixed.append(
                sum(mm(pick(left_split, 1, mine ^ known), held) for known, held in pieces.items())
            )
        mixed = jnp.concatenate(mixed, axis=1).astype(BF)
        update = mm_t(mixed, right_basis)
        master = pick(blocks, 0, my_blocks[slot])
        used = my_used[slot]
        first_list.append(first_step * used)
        second_list.append(second_step * used)
        weight_list.append((master - LEARN_RATE * (update + DECAY_WEIGHT * master)) * used)
    small_first_new = BETA_DECAY * small_first + (1.0 - BETA_DECAY) * small_grads
    small_second_new = BETA_DECAY * small_second + (1.0 - BETA_DECAY) * small_grads * small_grads
    small_weights = small_params - SMALL_RATE * small_first_new / (
        jnp.sqrt(small_second_new) + EPS_ADAM
    )
    return (
        layer_out,
        frames_grad,
        owned,
        jnp.stack(first_list),
        jnp.stack(second_list),
        jnp.stack(weight_list),
        small_grads,
        small_weights,
        small_first_new,
        small_second_new,
    )


def solution(mesh):
    placed = (
        P(("dp", "fsdp"), None, None),
        P(("dp", "fsdp"), None),
        P(("dp", "fsdp"), None, None),
        P(None, "fsdp", None),
        P(),
        P(),
        P("dp", "fsdp", None),
        P("dp", None, None),
        P("dp", "fsdp", None),
        P("dp", "fsdp", None),
        P(),
        P(),
    )
    return jax.shard_map(
        per_device,
        mesh=mesh,
        in_specs=placed,
        out_specs=(
            P(("dp", "fsdp"), None, None),
            P(("dp", "fsdp"), None, None),
            P("dp", "fsdp", None),
            P("dp", "fsdp", None),
            P("dp", "fsdp", None),
            P("dp", "fsdp", None),
            P(),
            P(),
            P(),
            P(),
        ),
        check_vma=False,
    )
```

```python
import jax
import jax.numpy as jnp
from jax import lax
from jax.experimental import pallas as pl
from jax.experimental.pallas import tpu as pltpu
from jax.sharding import Mesh
from jax.sharding import PartitionSpec as P

D = 1024
HEADS = 8
FF = 4096
KERNEL = 5
LENGTH = 512
HEAD = 128

EPS_NORM = 1e-05
EPS_ADAM = 1e-08
LEARN_RATE = 0.02
SMALL_RATE = 0.3
DECAY_WEIGHT = 0.01
BETA_DECAY = 0.5
MASKED = -1000000000.0
DP = ("dpz", "core")
AXES = (*DP, "fsdp")
BF = jnp.bfloat16
F32 = jnp.float32


def bits_of(size):
    return [1 << k for k in range(size.bit_length() - 1)]


def swap(value, dp_mask, fsdp_mask):
    n_dp, n_fsdp = lax.axis_size(DP), lax.axis_size("fsdp")
    pairs = [
        (d * n_fsdp + f, (d ^ dp_mask) * n_fsdp + (f ^ fsdp_mask))
        for d in range(n_dp)
        for f in range(n_fsdp)
    ]
    return lax.ppermute(value, AXES, pairs)


def swap_core(value):
    return swap(value, 1, 0)


def total(value):
    for mask in bits_of(lax.axis_size("fsdp")):
        value = value + swap(value, 0, mask)
    for mask in bits_of(lax.axis_size(DP)):
        value = value + swap(value, mask, 0)
    return value


class Route:
    def __init__(self, axis, flip):
        self.axis = axis
        if axis == "fsdp":
            self.size = lax.axis_size("fsdp")
            self.here = lax.axis_index("fsdp").astype(jnp.int32)
        else:
            self.size = lax.axis_size(DP) // 2
            self.here = lax.axis_index(DP).astype(jnp.int32) // 2
        self.bits = bits_of(self.size)
        if flip:
            self.bits = self.bits[::-1]
        self.differ = [0]
        for bit in self.bits[::-1]:
            self.differ = self.differ + [held | bit for held in self.differ]

    def trade(self, value, step):
        bit = self.bits[step]
        return swap(value, 0, bit) if self.axis == "fsdp" else swap(value, 2 * bit, 0)

    def indices(self):
        return self.here ^ jnp.array(self.differ, jnp.int32)


def after(value, *earlier):
    return lax.optimization_barrier((value, *earlier))[0]


def pick(value, axis, index):
    return lax.dynamic_index_in_dim(value, index, axis, keepdims=False)


def norm_apply(values, scale_row, shift_row):
    average = jnp.mean(values, axis=-1, keepdims=True)
    centered = values - average
    variance = jnp.mean(centered * centered, axis=-1, keepdims=True)
    return centered * lax.rsqrt(variance + EPS_NORM) * scale_row + shift_row


def swish(values):
    return values * jax.nn.sigmoid(values)


def depthwise(gated_rows, kernel_taps, segment_ids):
    length = gated_rows.shape[1]
    margin = KERNEL // 2
    padded = jnp.pad(gated_rows, ((0, 0), (margin, margin), (0, 0)))
    segment_pad = jnp.pad(segment_ids, ((0, 0), (margin, margin)), constant_values=-1)
    summed = jnp.zeros_like(gated_rows)
    for offset in range(KERNEL):
        matched = (segment_pad[:, offset : offset + length] == segment_ids)[:, :, None]
        summed = summed + kernel_taps[offset] * jnp.where(
            matched, padded[:, offset : offset + length], 0.0
        )
    return summed


def slot_tables(owners, groups, count_blocks):
    capacity = (count_blocks + groups - 1) // groups
    block_index = jnp.arange(count_blocks, dtype=jnp.int32)
    earlier = (owners[None, :] == owners[:, None]) & (block_index[None, :] < block_index[:, None])
    ranking = jnp.sum(earlier.astype(jnp.int32), axis=1)
    slot_of = owners * capacity + ranking
    return slot_of[None, :] == jnp.arange(capacity * groups, dtype=jnp.int32)[:, None]


def gated_conv(pre_a, pre_g, kernel_taps, segment_ids):
    rows_here = segment_ids.shape[0]
    gated_rows = pre_a * jax.nn.sigmoid(pre_g)
    shaped = gated_rows.reshape(rows_here, -1, gated_rows.shape[-1])
    return depthwise(shaped, kernel_taps, segment_ids).reshape(gated_rows.shape)


def masked_scores(queries, keys_row, segment_row):
    scores = jnp.einsum("qhe,khe->hqk", queries, keys_row, preferred_element_type=F32)
    matched = (segment_row[:, None] == segment_row[None, :])[None]
    return jnp.where(matched, scores, MASKED)


def attend_forward(arrays):
    queries, keys_row, values_row, segment_row = arrays
    scores = masked_scores(queries, keys_row, segment_row)
    highest = jnp.max(scores, axis=-1, keepdims=True)
    exponent = jnp.exp(scores - highest)
    summed = jnp.sum(exponent, axis=-1, keepdims=True)
    attention = (exponent / summed).astype(BF)
    context = jnp.einsum("hqk,khe->qhe", attention, values_row, preferred_element_type=F32)
    return (context, (highest + jnp.log(summed))[..., 0])


def attend_backward(arrays):
    queries, keys_row, values_row, segment_row, log_total, context_grad = arrays
    scores = masked_scores(queries, keys_row, segment_row)
    attention = jnp.exp(scores - log_total[..., None])
    attention_grad = jnp.einsum(
        "qhe,khe->hqk", context_grad, values_row, preferred_element_type=F32
    )
    score_grad = attention * (
        attention_grad - jnp.sum(attention_grad * attention, axis=-1, keepdims=True)
    )
    score_low = score_grad.astype(BF)
    query_grad = jnp.einsum("hqk,khe->qhe", score_low, keys_row, preferred_element_type=F32)
    key_grad = jnp.einsum("hqk,qhe->khe", score_low, queries, preferred_element_type=F32)
    value_grad = jnp.einsum(
        "hqk,qhe->khe", attention.astype(BF), context_grad, preferred_element_type=F32
    )
    return (query_grad, key_grad, value_grad)


def mm(left, right):
    return jnp.dot(left, right, preferred_element_type=F32)


def mm_t(left, right):
    return lax.dot_general(left, right, (((1,), (1,)), ((), ())), preferred_element_type=F32)


def t_mm(left, right):
    return lax.dot_general(left, right, (((0,), (0,)), ((), ())), preferred_element_type=F32)


def interleave(side, shard, fetched, arrived, local):
    count, n_shards, size, _ = fetched.shape

    def kernel(at_ref, fetched_ref, arrived_ref, local_ref, out_ref):
        near, here = at_ref[0], at_ref[1]
        for i in range(n_shards):
            at = pl.multiple_of((2 * i + near) * size, size)
            out_ref[0, pl.ds(at, size), :] = fetched_ref[0, i]
            at = pl.multiple_of((2 * (here ^ i) + 1 - near) * size, size)
            out_ref[0, pl.ds(at, size), :] = arrived_ref[0, i - 1] if i else local_ref[0]

    return pl.pallas_call(
        kernel,
        grid_spec=pltpu.PrefetchScalarGridSpec(
            num_scalar_prefetch=1,
            grid=(count,),
            in_specs=[
                pl.BlockSpec((1, n_shards, size, D), lambda b, s: (b, 0, 0, 0)),
                pl.BlockSpec((1, n_shards - 1, size, D), lambda b, s: (b, 0, 0, 0)),
                pl.BlockSpec((1, size, D), lambda b, s: (b, 0, 0)),
            ],
            out_specs=pl.BlockSpec((1, D, D), lambda b, s: (b, 0, 0)),
        ),
        out_shape=jax.ShapeDtypeStruct((count, D, D), BF),
        cost_estimate=pl.CostEstimate(
            flops=0, bytes_accessed=count * 4 * D * D, transcendentals=0
        ),
        name="interleave",
    )(jnp.stack([side, shard]), fetched, arrived, local)


def deal(chosen, used, parts):
    n_slots = chosen.shape[0]
    sizes = [part.shape[0] for part in parts]

    def kernel(chosen_ref, used_ref, *refs):
        *part_refs, out_ref, all_ref = refs
        at = 0
        for ref, size in zip(part_refs, sizes):
            all_ref[at : at + size] = ref[...]
            at += size
        for slot in range(n_slots):
            held = all_ref[chosen_ref[slot]].astype(F32)
            out_ref[slot] = (held * used_ref[slot].astype(F32)).astype(BF)

    return pl.pallas_call(
        kernel,
        in_specs=[pl.BlockSpec(memory_space=pltpu.SMEM)] * 2
        + [pl.BlockSpec(memory_space=pltpu.VMEM)] * len(parts),
        out_specs=pl.BlockSpec(memory_space=pltpu.VMEM),
        out_shape=jax.ShapeDtypeStruct((n_slots, *parts[0].shape[1:]), BF),
        scratch_shapes=[pltpu.VMEM((sum(sizes), *parts[0].shape[1:]), BF)],
        name="deal",
    )(chosen, used, *parts)


def regroup(starts, value, act=False, blocks=None):
    tokens = value.shape[0]
    blocks = list(range(value.shape[1] // D)) if blocks is None else blocks
    base, stride = blocks[0], (blocks[1] - blocks[0] if len(blocks) > 1 else 1)
    n_blocks = len(blocks)
    n_chunks = starts.shape[0]
    size = D // n_chunks
    if size % 128:
        value = jnp.concatenate([value[:, j * D : (j + 1) * D] for j in blocks], axis=1)
        value = swish(value.astype(F32)).astype(BF) if act else value
        split = value.reshape(tokens, n_blocks, n_chunks, size)
        return jnp.concatenate(
            [
                lax.dynamic_index_in_dim(split, starts[q], 2, keepdims=False).reshape(tokens, -1)
                for q in range(n_chunks)
            ],
            axis=1,
        )

    def kernel(starts_ref, value_ref, out_ref):
        block = pl.program_id(0)
        for place in range(n_chunks):
            at = pl.multiple_of(starts_ref[place] * size, size)
            held = value_ref[:, pl.ds(at, size)]
            if act:
                held = swish(held.astype(F32)).astype(BF)
            to = pl.multiple_of((place * n_blocks + block) * size, size)
            out_ref[:, pl.ds(to, size)] = held

    return pl.pallas_call(
        kernel,
        grid_spec=pltpu.PrefetchScalarGridSpec(
            num_scalar_prefetch=1,
            grid=(n_blocks,),
            in_specs=[pl.BlockSpec((tokens, D), lambda b, s: (0, base + stride * b))],
            out_specs=pl.BlockSpec((tokens, n_blocks * D), lambda b, s: (0, 0)),
        ),
        out_shape=jax.ShapeDtypeStruct((tokens, n_blocks * D), BF),
        cost_estimate=pl.CostEstimate(
            flops=0, bytes_accessed=4 * tokens * n_blocks * D, transcendentals=0
        ),
        name="regroup",
    )(starts, value)


def run(*tasks):
    got = [None] * len(tasks)
    left = list(tasks)
    while left:
        going, wants = [], []
        for task, arrived in zip(left, got):
            try:
                wants.append(task.send(arrived))
                going.append(task)
            except StopIteration:
                pass
        left, got = going, wants


def fetch(route, own, sink):
    sink[0] = own
    for step in range(len(route.bits)):
        known = list(sink)
        got = yield [route.trade(sink[place], step) for place in known]
        for place, piece in zip(known, got):
            sink[place + (route.size >> (step + 1))] = piece


def low_add(left, right):
    return (left.astype(F32) + right.astype(F32)).astype(BF)


def halve(route, kept, sent, sink, name):
    for step in range(len(route.bits)):
        arrived = yield route.trade(sent, step)
        if step + 1 == len(route.bits):
            sink[name] = kept + arrived.astype(F32) if kept.dtype == F32 else low_add(kept, arrived)
            return
        part = kept.shape[0] // 2
        sent = low_add(kept[part:], arrived[part:])
        kept = kept[:part].astype(F32) + arrived[:part].astype(F32) if kept.dtype == F32 else low_add(
            kept[:part], arrived[:part]
        )


def halve_dp(route, held, sink, name):
    count, sides, rows, _ = held.shape
    piece = rows // route.size
    core = lax.axis_index(DP) % 2
    indices = route.indices()
    parts = [
        lax.dynamic_slice(held, (0, 0, indices[place] * piece, 0), (count, sides, piece, D))
        for place in range(route.size)
    ]
    middle = route.size // 2
    yield from halve(route, jnp.stack(parts[:middle]), jnp.stack(parts[middle:]), sink, name)
    held = sink[name][0]
    if sides == 1:
        sink[name] = held[:, 0]
        return
    arrived = yield swap_core(pick(held, 1, 1 - core))
    sink[name] = [pick(held, 1, core), arrived]


def both(value):
    return jnp.concatenate([value, swap_core(value)], axis=0)


def across(partial):
    tokens = partial.shape[0] // 2
    return partial[:tokens] + swap_core(partial[tokens:])


def per_device(
    frames,
    segment_ids,
    out_grad,
    blocks,
    small_params,
    owners,
    left_bases,
    right_bases,
    block_first,
    block_second,
    small_first,
    small_second,
):
    rows_here = frames.shape[0]
    tokens = rows_here * LENGTH
    n_blocks = blocks.shape[0]
    rows_own = blocks.shape[1]
    scale_head = HEAD ** (-0.5)
    n_dp = lax.axis_size(DP)
    n_fsdp = lax.axis_size("fsdp")
    mine = lax.axis_index("fsdp")
    count_all = tokens * n_dp * n_fsdp
    core = lax.axis_index("core").astype(jnp.int32)
    dpz = lax.axis_index("dpz").astype(jnp.int32)
    fsdp = lax.axis_index("fsdp").astype(jnp.int32)
    half = rows_own // 2
    per_in = FF // D
    per_core = per_in // 2
    base_attn = 2 * per_in
    base_last = base_attn + 7
    routes = [Route("fsdp", False), Route("fsdp", True)]
    routes_dp = [Route("dp", False), Route("dp", True)]
    shards = [route.indices() for route in routes]

    def rows_of(low, count, side, size):
        return lax.dynamic_slice(blocks, (low, side * size, 0), (count, size, D)).astype(BF)

    def fetch_own(base):
        own = [rows_of(base + k * per_in + core * per_core, per_core, 0, rows_own) for k in (0, 1)]
        fetched = lax.all_gather(jnp.concatenate(own, axis=0), "fsdp", axis=1, tiled=True)
        return [fetched[j] for j in range(2 * per_core)]

    def fetch_shared(base):
        side = dpz % 2
        listed = []
        for k in (0, 1):
            at = base + k * per_in + core * per_core
            listed.append([rows_of(at, per_core, held, half) for held in (side, 1 - side)])
        own = jnp.concatenate([held for held, _ in listed], axis=0)
        fetched = lax.all_gather(own, "fsdp", axis=1, tiled=True)
        fetched = fetched.reshape(2, per_core, n_fsdp, half, D)
        result = []
        for k in (0, 1):
            away = jnp.stack(
                [pick(fetched[k], 1, shard) for shard in [fsdp ^ i for i in range(1, n_fsdp)]], axis=1
            )
            arrived = swap(away, 2, 0)
            result.append(interleave(side, fsdp, fetched[k], arrived, listed[k][1]))
        return [held[j] for held in result for j in range(per_core)]

    def fetch_half(low, high):
        own = rows_of(low, high - low, core, half)
        return lax.all_gather(own, ("fsdp", "core"), axis=1, tiled=True)

    gains = small_params[0:5]
    shifts = small_params[5:10]
    bn_gain = small_params[10]
    bn_shift = small_params[11]
    kernel_taps = small_params[12 : 12 + KERNEL]

    def feed_up(hidden, index, weights):
        normed, pullback = jax.vjp(norm_apply, hidden, gains[index], shifts[index])
        pair = both(normed.astype(BF))
        return [mm(pair, weights[j]).astype(BF) for j in range(per_core)], pullback, pair

    def feed_down(hidden, lifted, weights):
        acted = [swish(up.astype(F32)).astype(BF) for up in lifted]
        result = across(sum(mm(acted[j], weights[per_core + j]) for j in range(per_core)))
        return hidden + 0.5 * result, acted

    def feed_back(gradient, lifted, acted, normed_pair, weights):
        pair = both((0.5 * gradient).astype(BF))
        lows, grads_in, grads_out = [], [], []
        for j in range(per_core):
            acted_grad = mm_t(pair, weights[per_core + j])
            up = lifted[j].astype(F32)
            gate = jax.nn.sigmoid(up)
            lows.append((acted_grad * (gate * (1.0 + up * (1.0 - gate)))).astype(BF))
        normed_grad = across(sum(mm_t(lows[j], weights[j]) for j in range(per_core)))
        for j in range(per_core):
            grads_out.append(t_mm(acted[j], pair).astype(BF))
            grads_in.append(t_mm(normed_pair, lows[j]).astype(BF))
        listed = [held.reshape(n_fsdp, rows_own, D) for held in grads_in + grads_out]
        return normed_grad, jnp.stack(listed, axis=1)

    last = []

    def scatter(stacked):
        if last:
            stacked = after(stacked, last[-1])
        summed = lax.psum_scatter(stacked, "fsdp", scatter_dimension=0, tiled=True)
        last.append(lax.optimization_barrier(summed))
        return last[-1][0]

    def share(products, along_z):
        pieces = n_dp // 2
        shape = (n_fsdp, 2, pieces // 2, 2, half // pieces, D)
        split = [held.astype(BF).reshape(shape) for held in products]
        away = jnp.stack([pick(held, 1, 1 - core) for held in split], axis=1)
        arrived = swap_core(away)
        if not along_z:
            kept = jnp.stack([pick(held, 1, core) for held in split], axis=1)
            return low_add(kept, arrived).reshape(n_fsdp, len(split), half, D)
        side = dpz % 2

        def summed(which):
            kept = jnp.stack([pick(pick(held, 1, core), 2, which) for held in split], axis=1)
            return low_add(kept, pick(arrived, 3, which))

        sent, kept = summed(1 - side), summed(side)
        return low_add(kept, swap(sent, 2, 0))

    def spread_shared(held, name):
        for bit in bits_of(n_dp // 2)[1:]:
            count, left, rows, _ = held.shape
            parted = held.reshape(count, left // 2, 2, rows, D)
            which = (dpz // bit) % 2
            arrived = swap(pick(parted, 2, 1 - which), 2 * bit, 0)
            held = low_add(pick(parted, 2, which), arrived)
        sums[name] = held[:, 0]

    def spread_dp(held, sides, name):
        middle = (held.shape[0] + 1) // 2
        tasks = []
        for route, part, place in zip(routes_dp, (held[:middle], held[middle:]), "xy"):
            shaped = part.reshape(part.shape[0], sides, half, D)
            tasks.append(halve_dp(route, shaped, sums, name + place))
        run(*tasks)

    sums = {}
    weights1 = fetch_shared(0)
    weights_middle = fetch_half(base_attn, base_last)
    weights2 = fetch_own(base_last)
    w_attn, w_conv = weights_middle[:4], weights_middle[4:]
    start_x = frames.astype(F32).reshape(tokens, D)
    lifted1, ffn1_pullback, normed_pair1 = feed_up(start_x, 0, weights1)
    first_x, acted1 = feed_down(start_x, lifted1, weights1)
    normed, attn_pullback = jax.vjp(norm_apply, first_x, gains[1], shifts[1])
    attn_low = normed.astype(BF)
    split_shape = (rows_here, LENGTH, HEADS, HEAD)
    queries = (mm(attn_low, w_attn[0]) * scale_head).astype(BF).reshape(split_shape)
    keys_all = mm(attn_low, w_attn[1]).astype(BF).reshape(split_shape)
    values_all = mm(attn_low, w_attn[2]).astype(BF).reshape(split_shape)
    context, log_total = lax.map(attend_forward, (queries, keys_all, values_all, segment_ids))
    context_low = context.reshape(tokens, D).astype(BF)
    second_x = first_x + mm(context_low, w_attn[3])
    normed, conv_pullback = jax.vjp(norm_apply, second_x, gains[2], shifts[2])
    conv_low = normed.astype(BF)
    convolved, gated_pullback = jax.vjp(
        lambda pre_a, pre_g, taps_in: gated_conv(pre_a, pre_g, taps_in, segment_ids),
        mm(conv_low, w_conv[0]),
        mm(conv_low, w_conv[1]),
        kernel_taps,
    )
    stats = jnp.stack([jnp.sum(convolved, axis=0), jnp.sum(convolved * convolved, axis=0)])
    stats = total(stats)
    average = stats[0] / count_all
    inverse_dev = lax.rsqrt(stats[1] / count_all - average * average + EPS_NORM)
    standard = (convolved - average) * inverse_dev
    activated, bn_swish_pullback = jax.vjp(swish, standard * bn_gain + bn_shift)
    activated_low = activated.astype(BF)
    third_x = second_x + mm(activated_low, w_conv[2])
    lifted2, ffn2_pullback, normed_pair2 = feed_up(third_x, 3, weights2)
    fourth_x, acted2 = feed_down(third_x, lifted2, weights2)
    layer_value, final_pullback = jax.vjp(norm_apply, fourth_x, gains[4], shifts[4])
    layer_out = layer_value.astype(BF).reshape(rows_here, LENGTH, D)

    grad_x, final_gain, final_shift = final_pullback(out_grad.astype(F32).reshape(tokens, D))
    normed_grad, stacked = feed_back(grad_x, lifted2, acted2, normed_pair2, weights2)
    hidden_grad, ffn2_gain, ffn2_shift = ffn2_pullback(normed_grad)
    grad_x = grad_x + hidden_grad
    branch_low = grad_x.astype(BF)
    (bn_grad,) = bn_swish_pullback(mm_t(branch_low, w_conv[2]))
    bn_sums = jnp.stack([jnp.sum(bn_grad, axis=0), jnp.sum(bn_grad * standard, axis=0)])
    bn_sums = total(bn_sums)
    summed2 = scatter(stacked)
    grad_back = t_mm(activated_low, branch_low)
    shift_sum, gain_sum = bn_sums[0], bn_sums[1]
    conv_grad = (
        bn_gain
        * inverse_dev
        * (bn_grad - shift_sum / count_all - standard * (gain_sum / count_all))
    )
    grad_a, grad_g, taps_grad = gated_pullback(conv_grad)
    grad_a, grad_g = grad_a.astype(BF), grad_g.astype(BF)
    shared_conv = share([t_mm(conv_low, grad_a), t_mm(conv_low, grad_g), grad_back], False)
    summed_conv = scatter(shared_conv)
    part_x, conv_gain, conv_shift = conv_pullback(
        mm_t(grad_a, w_conv[0]) + mm_t(grad_g, w_conv[1])
    )
    grad_x = grad_x + part_x
    branch_low = grad_x.astype(BF)
    context_grad = mm_t(branch_low, w_attn[3]).astype(BF).reshape(split_shape)
    query_grad, key_grad, value_grad = lax.map(
        attend_backward, (queries, keys_all, values_all, segment_ids, log_total, context_grad)
    )
    query_low = (query_grad.reshape(tokens, D) * scale_head).astype(BF)
    key_low = key_grad.reshape(tokens, D).astype(BF)
    value_low = value_grad.reshape(tokens, D).astype(BF)
    grad_heads = [t_mm(attn_low, held) for held in (query_low, key_low, value_low)]
    shared_attn = share([*grad_heads, t_mm(context_low, branch_low)], True)
    part_x, attn_gain, attn_shift = attn_pullback(
        mm_t(query_low, w_attn[0]) + mm_t(key_low, w_attn[1]) + mm_t(value_low, w_attn[2])
    )
    grad_x = grad_x + part_x
    normed_grad, stacked = feed_back(grad_x, lifted1, acted1, normed_pair1, weights1)
    summed1 = scatter(stacked)
    summed_attn = scatter(shared_attn)
    hidden_grad, ffn1_gain, ffn1_shift = ffn1_pullback(normed_grad)
    grad_x = grad_x + hidden_grad
    frames_grad = grad_x.reshape(rows_here, LENGTH, D)
    local_small = jnp.concatenate(
        [
            jnp.stack([ffn1_gain, attn_gain, conv_gain, ffn2_gain, final_gain]),
            jnp.stack([ffn1_shift, attn_shift, conv_shift, ffn2_shift, final_shift]),
            taps_grad,
        ],
        axis=0,
    )
    spread_dp(summed2, 2, "ffn2")
    spread_dp(summed_conv, 1, "conv")
    summed1 = after(summed1, *[sums[name + place] for name in ("ffn2", "conv") for place in "xy"])
    spread_dp(summed1, 2, "ffn1")
    summed_attn = after(summed_attn, *[sums["ffn1" + place] for place in "xy"])
    spread_shared(summed_attn, "attn")
    summed_small = total(local_small)
    small_grads = jnp.concatenate(
        [summed_small[0:10], gain_sum[None], shift_sum[None], summed_small[10:]], axis=0
    )

    parts, places = [], []
    for name in ("ffn1", "middle", "ffn2"):
        base = sum(part.shape[0] for part in parts)
        if name == "middle":
            parts += [sums["attn"], sums["convx"], sums["convy"]]
            places.append(base + jnp.arange(base_last - base_attn, dtype=jnp.int32))
            continue
        (in_mine, in_other), (out_mine, out_other) = sums[name + "x"], sums[name + "y"]
        parts += [in_mine, out_mine, in_other, out_other]
        index = jnp.arange(2 * per_in, dtype=jnp.int32)
        is_out, index = index // per_in, index % per_in
        away = (index // per_core != core).astype(jnp.int32)
        places.append(base + (2 * away + is_out) * per_core + index % per_core)
    places = jnp.concatenate(places)
    capacity = (n_blocks + n_dp - 1) // n_dp
    matches = slot_tables(owners, n_dp, n_blocks).astype(jnp.int32)
    slot_block = jnp.sum(matches * jnp.arange(n_blocks, dtype=jnp.int32)[None], axis=1)
    slot_used = jnp.sum(matches, axis=1)
    piece = half // (n_dp // 2)
    slot_place = jnp.sum(matches * places[None], axis=1)
    sent = deal(slot_place, slot_used, parts).reshape(n_dp, capacity, piece, D)
    came = lax.all_to_all(sent, DP, 0, 0, tiled=False)
    came = came.reshape(n_dp // 2, 2, capacity, piece, D).transpose(2, 1, 0, 3, 4)
    owned_list = came.reshape(capacity, rows_own, D)

    dp_here = lax.axis_index(DP)
    my_blocks = lax.dynamic_slice_in_dim(slot_block, dp_here * capacity, capacity)
    my_used = lax.dynamic_slice_in_dim(slot_used, dp_here * capacity, capacity).astype(F32)
    rotated_list, weight_list = [], []
    sides = [slice(0, D // 2), slice(D // 2, D)]
    for slot in range(capacity):
        right_basis = right_bases[slot].astype(BF)
        left_low = left_bases[slot].astype(BF)
        lefts = [regroup(held, left_low) for held in shards]
        product = mm(owned_list[slot], right_basis).astype(BF)
        sink = {}
        run(
            *[
                halve(
                    routes[i],
                    t_mm(lefts[i][:, : D // 2], product[:, sides[i]]),
                    t_mm(lefts[i][:, D // 2 :], product[:, sides[i]]).astype(BF),
                    sink,
                    i,
                )
                for i in (0, 1)
            ]
        )
        sinks = [{}, {}]
        tasks = []
        for i in (0, 1):
            first_step = 0.5 * block_first[slot][:, sides[i]] + 0.5 * sink[i]
            second_step = 0.5 * block_second[slot][:, sides[i]] + 0.5 * sink[i] * sink[i]
            direction = (first_step / (jnp.sqrt(second_step) + EPS_ADAM)).astype(BF)
            tasks.append(fetch(routes[i], direction, sinks[i]))
        run(*tasks)
        rotated_list.append(jnp.concatenate([sink[0], sink[1]], axis=1))
        mixed = [
            mm(
                lefts[i], jnp.concatenate([sinks[i][place] for place in range(n_fsdp)], axis=0)
            ).astype(BF)
            for i in (0, 1)
        ]
        update = mm_t(jnp.concatenate(mixed, axis=1), right_basis)
        master = pick(blocks, 0, my_blocks[slot])
        weight_list.append(master - LEARN_RATE * (update + DECAY_WEIGHT * master))
    used = my_used[:, None, None]
    rotated = jnp.stack(rotated_list)
    first_step = BETA_DECAY * block_first + (1.0 - BETA_DECAY) * rotated
    second_step = BETA_DECAY * block_second + (1.0 - BETA_DECAY) * rotated * rotated
    small_first_new = BETA_DECAY * small_first + (1.0 - BETA_DECAY) * small_grads
    small_second_new = BETA_DECAY * small_second + (1.0 - BETA_DECAY) * small_grads * small_grads
    small_weights = small_params - SMALL_RATE * small_first_new / (
        jnp.sqrt(small_second_new) + EPS_ADAM
    )
    return (
        layer_out,
        frames_grad,
        owned_list.astype(F32),
        first_step * used,
        second_step * used,
        jnp.stack(weight_list) * used,
        small_grads,
        small_weights,
        small_first_new,
        small_second_new,
    )


def solution(mesh):
    n_dp, n_fsdp = mesh.shape["dp"], mesh.shape["fsdp"]
    finer = Mesh(mesh.devices.reshape(n_dp // 2, 2, n_fsdp), AXES)
    placed = (
        P(AXES, None, None),
        P(AXES, None),
        P(AXES, None, None),
        P(None, "fsdp", None),
        P(),
        P(),
        P(DP, "fsdp", None),
        P(DP, None, None),
        P(DP, "fsdp", None),
        P(DP, "fsdp", None),
        P(),
        P(),
    )
    return jax.shard_map(
        per_device,
        mesh=finer,
        in_specs=placed,
        out_specs=(
            P(AXES, None, None),
            P(AXES, None, None),
            P(DP, "fsdp", None),
            P(DP, "fsdp", None),
            P(DP, "fsdp", None),
            P(DP, "fsdp", None),
            P(),
            P(),
            P(),
            P(),
        ),
        check_vma=False,
    )
```

```python
import jax
import jax.numpy as jnp
from jax import lax
from jax.experimental import pallas as pl
from jax.experimental.pallas import tpu as pltpu
from jax.sharding import Mesh
from jax.sharding import PartitionSpec as P

D = 1024
HEADS = 8
FF = 4096
KERNEL = 5
LENGTH = 512
HEAD = 128

EPS_NORM = 1e-05
EPS_ADAM = 1e-08
LEARN_RATE = 0.02
SMALL_RATE = 0.3
DECAY_WEIGHT = 0.01
BETA_DECAY = 0.5
MASKED = -1000000000.0
DP = ("dpz", "core")
AXES = (*DP, "fsdp")
BF = jnp.bfloat16
F32 = jnp.float32


def bits_of(size):
    return [1 << k for k in range(size.bit_length() - 1)]


def swap(value, dp_mask, fsdp_mask):
    n_dp, n_fsdp = lax.axis_size(DP), lax.axis_size("fsdp")
    pairs = [
        (d * n_fsdp + f, (d ^ dp_mask) * n_fsdp + (f ^ fsdp_mask))
        for d in range(n_dp)
        for f in range(n_fsdp)
    ]
    return lax.ppermute(value, AXES, pairs)


def swap_core(value):
    return swap(value, 1, 0)


def total(value):
    for mask in bits_of(lax.axis_size("fsdp")):
        value = value + swap(value, 0, mask)
    for mask in bits_of(lax.axis_size(DP)):
        value = value + swap(value, mask, 0)
    return value


class Route:
    def __init__(self, axis, flip):
        self.axis = axis
        if axis == "fsdp":
            self.size = lax.axis_size("fsdp")
            self.here = lax.axis_index("fsdp").astype(jnp.int32)
        else:
            self.size = lax.axis_size(DP) // 2
            self.here = lax.axis_index(DP).astype(jnp.int32) // 2
        self.bits = bits_of(self.size)
        if flip:
            self.bits = self.bits[::-1]
        self.differ = [0]
        for bit in self.bits[::-1]:
            self.differ = self.differ + [held | bit for held in self.differ]

    def trade(self, value, step):
        bit = self.bits[step]
        return swap(value, 0, bit) if self.axis == "fsdp" else swap(value, 2 * bit, 0)

    def indices(self):
        return self.here ^ jnp.array(self.differ, jnp.int32)


def after(value, *earlier):
    return lax.optimization_barrier((value, *earlier))[0]


def pick(value, axis, index):
    return lax.dynamic_index_in_dim(value, index, axis, keepdims=False)


def norm_apply(values, scale_row, shift_row):
    average = jnp.mean(values, axis=-1, keepdims=True)
    centered = values - average
    variance = jnp.mean(centered * centered, axis=-1, keepdims=True)
    return centered * lax.rsqrt(variance + EPS_NORM) * scale_row + shift_row


def swish(values):
    return values * jax.nn.sigmoid(values)


def depthwise(gated_rows, kernel_taps, segment_ids):
    length = gated_rows.shape[1]
    margin = KERNEL // 2
    padded = jnp.pad(gated_rows, ((0, 0), (margin, margin), (0, 0)))
    segment_pad = jnp.pad(segment_ids, ((0, 0), (margin, margin)), constant_values=-1)
    summed = jnp.zeros_like(gated_rows)
    for offset in range(KERNEL):
        matched = (segment_pad[:, offset : offset + length] == segment_ids)[:, :, None]
        summed = summed + kernel_taps[offset] * jnp.where(
            matched, padded[:, offset : offset + length], 0.0
        )
    return summed


def slot_tables(owners, groups, count_blocks):
    capacity = (count_blocks + groups - 1) // groups
    block_index = jnp.arange(count_blocks, dtype=jnp.int32)
    earlier = (owners[None, :] == owners[:, None]) & (block_index[None, :] < block_index[:, None])
    ranking = jnp.sum(earlier.astype(jnp.int32), axis=1)
    slot_of = owners * capacity + ranking
    return slot_of[None, :] == jnp.arange(capacity * groups, dtype=jnp.int32)[:, None]


def gated_conv(pre_a, pre_g, kernel_taps, segment_ids):
    rows_here = segment_ids.shape[0]
    gated_rows = pre_a * jax.nn.sigmoid(pre_g)
    shaped = gated_rows.reshape(rows_here, -1, gated_rows.shape[-1])
    return depthwise(shaped, kernel_taps, segment_ids).reshape(gated_rows.shape)


def masked_scores(queries, keys_row, segment_row):
    scores = jnp.einsum("qhe,khe->hqk", queries, keys_row, preferred_element_type=F32)
    matched = (segment_row[:, None] == segment_row[None, :])[None]
    return jnp.where(matched, scores, MASKED)


def attend_forward(arrays):
    queries, keys_row, values_row, segment_row = arrays
    scores = masked_scores(queries, keys_row, segment_row)
    highest = jnp.max(scores, axis=-1, keepdims=True)
    exponent = jnp.exp(scores - highest)
    summed = jnp.sum(exponent, axis=-1, keepdims=True)
    attention = (exponent / summed).astype(BF)
    context = jnp.einsum("hqk,khe->qhe", attention, values_row, preferred_element_type=F32)
    return (context, (highest + jnp.log(summed))[..., 0])


def attend_backward(arrays):
    queries, keys_row, values_row, segment_row, log_total, context_grad = arrays
    scores = masked_scores(queries, keys_row, segment_row)
    attention = jnp.exp(scores - log_total[..., None])
    attention_grad = jnp.einsum(
        "qhe,khe->hqk", context_grad, values_row, preferred_element_type=F32
    )
    score_grad = attention * (
        attention_grad - jnp.sum(attention_grad * attention, axis=-1, keepdims=True)
    )
    score_low = score_grad.astype(BF)
    query_grad = jnp.einsum("hqk,khe->qhe", score_low, keys_row, preferred_element_type=F32)
    key_grad = jnp.einsum("hqk,qhe->khe", score_low, queries, preferred_element_type=F32)
    value_grad = jnp.einsum(
        "hqk,qhe->khe", attention.astype(BF), context_grad, preferred_element_type=F32
    )
    return (query_grad, key_grad, value_grad)


def mm(left, right):
    return jnp.dot(left, right, preferred_element_type=F32)


def mm_t(left, right):
    return lax.dot_general(left, right, (((1,), (1,)), ((), ())), preferred_element_type=F32)


def t_mm(left, right):
    return lax.dot_general(left, right, (((0,), (0,)), ((), ())), preferred_element_type=F32)


def interleave(side, shard, fetched, arrived, local):
    count, n_shards, size, _ = fetched.shape

    def kernel(at_ref, fetched_ref, arrived_ref, local_ref, out_ref):
        near, here = at_ref[0], at_ref[1]
        for i in range(n_shards):
            at = pl.multiple_of((2 * i + near) * size, size)
            out_ref[0, pl.ds(at, size), :] = fetched_ref[0, i]
            at = pl.multiple_of((2 * (here ^ i) + 1 - near) * size, size)
            out_ref[0, pl.ds(at, size), :] = arrived_ref[0, i - 1] if i else local_ref[0]

    return pl.pallas_call(
        kernel,
        grid_spec=pltpu.PrefetchScalarGridSpec(
            num_scalar_prefetch=1,
            grid=(count,),
            in_specs=[
                pl.BlockSpec((1, n_shards, size, D), lambda b, s: (b, 0, 0, 0)),
                pl.BlockSpec((1, n_shards - 1, size, D), lambda b, s: (b, 0, 0, 0)),
                pl.BlockSpec((1, size, D), lambda b, s: (b, 0, 0)),
            ],
            out_specs=pl.BlockSpec((1, D, D), lambda b, s: (b, 0, 0)),
        ),
        out_shape=jax.ShapeDtypeStruct((count, D, D), BF),
        cost_estimate=pl.CostEstimate(
            flops=0, bytes_accessed=count * 4 * D * D, transcendentals=0
        ),
        name="interleave",
    )(jnp.stack([side, shard]), fetched, arrived, local)


def deal(chosen, used, parts):
    n_slots = chosen.shape[0]
    sizes = [part.shape[0] for part in parts]

    def kernel(chosen_ref, used_ref, *refs):
        *part_refs, out_ref, all_ref = refs
        at = 0
        for ref, size in zip(part_refs, sizes):
            all_ref[at : at + size] = ref[...]
            at += size
        for slot in range(n_slots):
            held = all_ref[chosen_ref[slot]].astype(F32)
            out_ref[slot] = (held * used_ref[slot].astype(F32)).astype(BF)

    return pl.pallas_call(
        kernel,
        in_specs=[pl.BlockSpec(memory_space=pltpu.SMEM)] * 2
        + [pl.BlockSpec(memory_space=pltpu.VMEM)] * len(parts),
        out_specs=pl.BlockSpec(memory_space=pltpu.VMEM),
        out_shape=jax.ShapeDtypeStruct((n_slots, *parts[0].shape[1:]), BF),
        scratch_shapes=[pltpu.VMEM((sum(sizes), *parts[0].shape[1:]), BF)],
        name="deal",
    )(chosen, used, *parts)


def regroup(starts, value, act=False, blocks=None):
    tokens = value.shape[0]
    blocks = list(range(value.shape[1] // D)) if blocks is None else blocks
    base, stride = blocks[0], (blocks[1] - blocks[0] if len(blocks) > 1 else 1)
    n_blocks = len(blocks)
    n_chunks = starts.shape[0]
    size = D // n_chunks
    if size % 128:
        value = jnp.concatenate([value[:, j * D : (j + 1) * D] for j in blocks], axis=1)
        value = swish(value.astype(F32)).astype(BF) if act else value
        split = value.reshape(tokens, n_blocks, n_chunks, size)
        return jnp.concatenate(
            [
                lax.dynamic_index_in_dim(split, starts[q], 2, keepdims=False).reshape(tokens, -1)
                for q in range(n_chunks)
            ],
            axis=1,
        )

    def kernel(starts_ref, value_ref, out_ref):
        block = pl.program_id(0)
        for place in range(n_chunks):
            at = pl.multiple_of(starts_ref[place] * size, size)
            held = value_ref[:, pl.ds(at, size)]
            if act:
                held = swish(held.astype(F32)).astype(BF)
            to = pl.multiple_of((place * n_blocks + block) * size, size)
            out_ref[:, pl.ds(to, size)] = held

    return pl.pallas_call(
        kernel,
        grid_spec=pltpu.PrefetchScalarGridSpec(
            num_scalar_prefetch=1,
            grid=(n_blocks,),
            in_specs=[pl.BlockSpec((tokens, D), lambda b, s: (0, base + stride * b))],
            out_specs=pl.BlockSpec((tokens, n_blocks * D), lambda b, s: (0, 0)),
        ),
        out_shape=jax.ShapeDtypeStruct((tokens, n_blocks * D), BF),
        cost_estimate=pl.CostEstimate(
            flops=0, bytes_accessed=4 * tokens * n_blocks * D, transcendentals=0
        ),
        name="regroup",
    )(starts, value)


def run(*tasks):
    got = [None] * len(tasks)
    left = list(tasks)
    while left:
        going, wants = [], []
        for task, arrived in zip(left, got):
            try:
                wants.append(task.send(arrived))
                going.append(task)
            except StopIteration:
                pass
        left, got = going, wants


def fetch(route, own, sink):
    sink[0] = own
    for step in range(len(route.bits)):
        known = list(sink)
        got = yield [route.trade(sink[place], step) for place in known]
        for place, piece in zip(known, got):
            sink[place + (route.size >> (step + 1))] = piece


def low_add(left, right):
    return (left.astype(F32) + right.astype(F32)).astype(BF)


def halve(route, kept, sent, sink, name):
    for step in range(len(route.bits)):
        arrived = yield route.trade(sent, step)
        if step + 1 == len(route.bits):
            sink[name] = kept + arrived.astype(F32) if kept.dtype == F32 else low_add(kept, arrived)
            return
        part = kept.shape[0] // 2
        sent = low_add(kept[part:], arrived[part:])
        kept = kept[:part].astype(F32) + arrived[:part].astype(F32) if kept.dtype == F32 else low_add(
            kept[:part], arrived[:part]
        )


def halve_dp(route, held, sink, name):
    count, sides, rows, _ = held.shape
    piece = rows // route.size
    core = lax.axis_index(DP) % 2
    indices = route.indices()
    parts = [
        lax.dynamic_slice(held, (0, 0, indices[place] * piece, 0), (count, sides, piece, D))
        for place in range(route.size)
    ]
    middle = route.size // 2
    yield from halve(route, jnp.stack(parts[:middle]), jnp.stack(parts[middle:]), sink, name)
    held = sink[name][0]
    if sides == 1:
        sink[name] = held[:, 0]
        return
    arrived = yield swap_core(pick(held, 1, 1 - core))
    sink[name] = [pick(held, 1, core), arrived]


def both(value):
    return jnp.concatenate([value, swap_core(value)], axis=0)


def across(partial):
    tokens = partial.shape[0] // 2
    return partial[:tokens] + swap_core(partial[tokens:])


def per_device(
    frames,
    segment_ids,
    out_grad,
    blocks,
    small_params,
    owners,
    left_bases,
    right_bases,
    block_first,
    block_second,
    small_first,
    small_second,
):
    rows_here = frames.shape[0]
    tokens = rows_here * LENGTH
    n_blocks = blocks.shape[0]
    rows_own = blocks.shape[1]
    scale_head = HEAD ** (-0.5)
    n_dp = lax.axis_size(DP)
    n_fsdp = lax.axis_size("fsdp")
    mine = lax.axis_index("fsdp")
    count_all = tokens * n_dp * n_fsdp
    core = lax.axis_index("core").astype(jnp.int32)
    dpz = lax.axis_index("dpz").astype(jnp.int32)
    fsdp = lax.axis_index("fsdp").astype(jnp.int32)
    half = rows_own // 2
    per_in = FF // D
    per_core = per_in // 2
    base_attn = 2 * per_in
    base_last = base_attn + 7
    routes = [Route("fsdp", False), Route("fsdp", True)]
    routes_dp = [Route("dp", False), Route("dp", True)]
    shards = [route.indices() for route in routes]

    def rows_of(low, count, side, size):
        return lax.dynamic_slice(blocks, (low, side * size, 0), (count, size, D)).astype(BF)

    def own_share(base):
        own = [rows_of(base + k * per_in + core * per_core, per_core, 0, rows_own) for k in (0, 1)]
        return jnp.concatenate(own, axis=0)

    def fetch_own(own):
        fetched = lax.all_gather(own, "fsdp", axis=1, tiled=True)
        return [fetched[j] for j in range(2 * per_core)]

    def fetch_shared(base):
        side = dpz % 2
        listed = []
        for k in (0, 1):
            at = base + k * per_in + core * per_core
            listed.append([rows_of(at, per_core, held, half) for held in (side, 1 - side)])
        own = jnp.concatenate([held for held, _ in listed], axis=0)
        fetched = lax.all_gather(own, "fsdp", axis=1, tiled=True)
        fetched = fetched.reshape(2, per_core, n_fsdp, half, D)
        result = []
        for k in (0, 1):
            away = jnp.stack(
                [pick(fetched[k], 1, shard) for shard in [fsdp ^ i for i in range(1, n_fsdp)]], axis=1
            )
            arrived = swap(away, 2, 0)
            result.append(interleave(side, fsdp, fetched[k], arrived, listed[k][1]))
        return [held[j] for held in result for j in range(per_core)]

    def fetch_half(low, high):
        own = rows_of(low, high - low, core, half)
        return lax.all_gather(own, ("fsdp", "core"), axis=1, tiled=True)

    gains = small_params[0:5]
    shifts = small_params[5:10]
    bn_gain = small_params[10]
    bn_shift = small_params[11]
    kernel_taps = small_params[12 : 12 + KERNEL]

    def feed_up(hidden, index, weights):
        normed, pullback = jax.vjp(norm_apply, hidden, gains[index], shifts[index])
        pair = both(normed.astype(BF))
        return [mm(pair, weights[j]).astype(BF) for j in range(per_core)], pullback, pair

    def feed_down(hidden, lifted, weights):
        acted = [swish(up.astype(F32)).astype(BF) for up in lifted]
        result = across(sum(mm(acted[j], weights[per_core + j]) for j in range(per_core)))
        return hidden + 0.5 * result, acted

    def feed_back(gradient, lifted, acted, normed_pair, weights):
        pair = both((0.5 * gradient).astype(BF))
        lows, grads_in, grads_out = [], [], []
        for j in range(per_core):
            acted_grad = mm_t(pair, weights[per_core + j])
            up = lifted[j].astype(F32)
            gate = jax.nn.sigmoid(up)
            lows.append((acted_grad * (gate * (1.0 + up * (1.0 - gate)))).astype(BF))
        for j in range(per_core):
            grads_out.append(t_mm(acted[j], pair).astype(BF))
            grads_in.append(t_mm(normed_pair, lows[j]).astype(BF))
        listed = [held.reshape(n_fsdp, rows_own, D) for held in grads_in + grads_out]
        stacked = jnp.stack(listed, axis=1)
        lows, stacked = lax.optimization_barrier((lows, stacked))
        return across(sum(mm_t(lows[j], weights[j]) for j in range(per_core))), stacked

    last = []

    def scatter(stacked):
        if last:
            stacked = after(stacked, last[-1])
        summed = lax.psum_scatter(stacked, "fsdp", scatter_dimension=0, tiled=True)
        last.append(lax.optimization_barrier(summed))
        return last[-1][0]

    def share(products):
        split = [held.astype(BF).reshape(n_fsdp, 2, half, D) for held in products]
        arrived = swap_core(jnp.stack([pick(held, 1, 1 - core) for held in split], axis=1))
        kept = jnp.stack([pick(held, 1, core) for held in split], axis=1)
        return low_add(kept, arrived)

    def spread_dp(held, sides, name):
        middle = (held.shape[0] + 1) // 2
        tasks = []
        for route, part, place in zip(routes_dp, (held[:middle], held[middle:]), "xy"):
            shaped = part.reshape(part.shape[0], sides, half, D)
            tasks.append(halve_dp(route, shaped, sums, name + place))
        run(*tasks)

    sums = {}
    weights1 = fetch_shared(0)
    weights_middle = fetch_half(base_attn, base_last)
    start_x = frames.astype(F32).reshape(tokens, D)
    start_x, own2 = lax.optimization_barrier((start_x, own_share(base_last)))
    weights2 = fetch_own(own2)
    w_attn, w_conv = weights_middle[:4], weights_middle[4:]
    lifted1, ffn1_pullback, normed_pair1 = feed_up(start_x, 0, weights1)
    first_x, acted1 = feed_down(start_x, lifted1, weights1)
    normed, attn_pullback = jax.vjp(norm_apply, first_x, gains[1], shifts[1])
    attn_low = normed.astype(BF)
    split_shape = (rows_here, LENGTH, HEADS, HEAD)
    queries = (mm(attn_low, w_attn[0]) * scale_head).astype(BF).reshape(split_shape)
    keys_all = mm(attn_low, w_attn[1]).astype(BF).reshape(split_shape)
    values_all = mm(attn_low, w_attn[2]).astype(BF).reshape(split_shape)
    context, log_total = lax.map(attend_forward, (queries, keys_all, values_all, segment_ids))
    context_low = context.reshape(tokens, D).astype(BF)
    second_x = first_x + mm(context_low, w_attn[3])
    normed, conv_pullback = jax.vjp(norm_apply, second_x, gains[2], shifts[2])
    conv_low = normed.astype(BF)
    convolved, gated_pullback = jax.vjp(
        lambda pre_a, pre_g, taps_in: gated_conv(pre_a, pre_g, taps_in, segment_ids),
        mm(conv_low, w_conv[0]),
        mm(conv_low, w_conv[1]),
        kernel_taps,
    )
    stats = jnp.stack([jnp.sum(convolved, axis=0), jnp.sum(convolved * convolved, axis=0)])
    stats = total(stats)
    average = stats[0] / count_all
    inverse_dev = lax.rsqrt(stats[1] / count_all - average * average + EPS_NORM)
    standard = (convolved - average) * inverse_dev
    activated, bn_swish_pullback = jax.vjp(swish, standard * bn_gain + bn_shift)
    activated_low = activated.astype(BF)
    third_x = second_x + mm(activated_low, w_conv[2])
    lifted2, ffn2_pullback, normed_pair2 = feed_up(third_x, 3, weights2)
    fourth_x, acted2 = feed_down(third_x, lifted2, weights2)
    layer_value, final_pullback = jax.vjp(norm_apply, fourth_x, gains[4], shifts[4])
    layer_out = layer_value.astype(BF).reshape(rows_here, LENGTH, D)

    grad_x, final_gain, final_shift = final_pullback(out_grad.astype(F32).reshape(tokens, D))
    normed_grad, stacked = feed_back(grad_x, lifted2, acted2, normed_pair2, weights2)
    hidden_grad, ffn2_gain, ffn2_shift = ffn2_pullback(normed_grad)
    grad_x = grad_x + hidden_grad
    branch_low = grad_x.astype(BF)
    (bn_grad,) = bn_swish_pullback(mm_t(branch_low, w_conv[2]))
    bn_sums = jnp.stack([jnp.sum(bn_grad, axis=0), jnp.sum(bn_grad * standard, axis=0)])
    bn_sums = total(bn_sums)
    summed2 = scatter(stacked)
    grad_back = t_mm(activated_low, branch_low)
    shift_sum, gain_sum = bn_sums[0], bn_sums[1]
    conv_grad = (
        bn_gain
        * inverse_dev
        * (bn_grad - shift_sum / count_all - standard * (gain_sum / count_all))
    )
    grad_a, grad_g, taps_grad = gated_pullback(conv_grad)
    grad_a, grad_g = grad_a.astype(BF), grad_g.astype(BF)
    shared_conv = share([t_mm(conv_low, grad_a), t_mm(conv_low, grad_g), grad_back])
    summed_conv = scatter(shared_conv)
    part_x, conv_gain, conv_shift = conv_pullback(
        mm_t(grad_a, w_conv[0]) + mm_t(grad_g, w_conv[1])
    )
    grad_x = grad_x + part_x
    branch_low = grad_x.astype(BF)
    context_grad = mm_t(branch_low, w_attn[3]).astype(BF).reshape(split_shape)
    query_grad, key_grad, value_grad = lax.map(
        attend_backward, (queries, keys_all, values_all, segment_ids, log_total, context_grad)
    )
    query_low = (query_grad.reshape(tokens, D) * scale_head).astype(BF)
    key_low = key_grad.reshape(tokens, D).astype(BF)
    value_low = value_grad.reshape(tokens, D).astype(BF)
    query_low, key_low, value_low, summed2 = lax.optimization_barrier(
        (query_low, key_low, value_low, summed2)
    )
    grad_heads = [t_mm(attn_low, held) for held in (query_low, key_low, value_low)]
    grad_proj = t_mm(context_low, branch_low)
    part_x, attn_gain, attn_shift = attn_pullback(
        mm_t(query_low, w_attn[0]) + mm_t(key_low, w_attn[1]) + mm_t(value_low, w_attn[2])
    )
    grad_x = grad_x + part_x
    normed_grad, stacked = feed_back(grad_x, lifted1, acted1, normed_pair1, weights1)
    summed1 = scatter(stacked)
    spread_dp(summed2, 2, "ffn2")
    spread_dp(summed_conv, 1, "conv")
    summed_attn = scatter(
        after(
            share([*grad_heads, grad_proj]),
            *[sums[name + place] for name in ("ffn2", "conv") for place in "xy"],
        )
    )
    hidden_grad, ffn1_gain, ffn1_shift = ffn1_pullback(normed_grad)
    grad_x = grad_x + hidden_grad
    frames_grad = grad_x.reshape(rows_here, LENGTH, D)
    local_small = jnp.concatenate(
        [
            jnp.stack([ffn1_gain, attn_gain, conv_gain, ffn2_gain, final_gain]),
            jnp.stack([ffn1_shift, attn_shift, conv_shift, ffn2_shift, final_shift]),
            taps_grad,
        ],
        axis=0,
    )
    spread_dp(summed1, 2, "ffn1")
    summed_attn = after(summed_attn, *[sums["ffn1" + place] for place in "xy"])
    spread_dp(summed_attn, 1, "attn")
    summed_small = total(local_small)
    small_grads = jnp.concatenate(
        [summed_small[0:10], gain_sum[None], shift_sum[None], summed_small[10:]], axis=0
    )

    parts, places = [], []
    for name in ("ffn1", "middle", "ffn2"):
        base = sum(part.shape[0] for part in parts)
        if name == "middle":
            parts += [sums[name + place] for name in ("attn", "conv") for place in "xy"]
            places.append(base + jnp.arange(base_last - base_attn, dtype=jnp.int32))
            continue
        (in_mine, in_other), (out_mine, out_other) = sums[name + "x"], sums[name + "y"]
        parts += [in_mine, out_mine, in_other, out_other]
        index = jnp.arange(2 * per_in, dtype=jnp.int32)
        is_out, index = index // per_in, index % per_in
        away = (index // per_core != core).astype(jnp.int32)
        places.append(base + (2 * away + is_out) * per_core + index % per_core)
    places = jnp.concatenate(places)
    capacity = (n_blocks + n_dp - 1) // n_dp
    matches = slot_tables(owners, n_dp, n_blocks).astype(jnp.int32)
    slot_block = jnp.sum(matches * jnp.arange(n_blocks, dtype=jnp.int32)[None], axis=1)
    slot_used = jnp.sum(matches, axis=1)
    piece = half // (n_dp // 2)
    slot_place = jnp.sum(matches * places[None], axis=1)
    parts, frames_grad = lax.optimization_barrier((parts, frames_grad))
    sent = deal(slot_place, slot_used, parts).reshape(n_dp, capacity, piece, D)
    came = lax.all_to_all(sent, DP, 0, 0, tiled=False)
    came = came.reshape(n_dp // 2, 2, capacity, piece, D).transpose(2, 1, 0, 3, 4)
    owned_list = came.reshape(capacity, rows_own, D)

    dp_here = lax.axis_index(DP)
    my_blocks = lax.dynamic_slice_in_dim(slot_block, dp_here * capacity, capacity)
    my_used = lax.dynamic_slice_in_dim(slot_used, dp_here * capacity, capacity).astype(F32)
    rotated_list, weight_list = [], []
    sides = [slice(0, D // 2), slice(D // 2, D)]
    for slot in range(capacity):
        right_basis = right_bases[slot].astype(BF)
        left_low = left_bases[slot].astype(BF)
        lefts = [regroup(held, left_low) for held in shards]
        product = mm(owned_list[slot], right_basis).astype(BF)
        sink = {}
        run(
            *[
                halve(
                    routes[i],
                    t_mm(lefts[i][:, : D // 2], product[:, sides[i]]),
                    t_mm(lefts[i][:, D // 2 :], product[:, sides[i]]).astype(BF),
                    sink,
                    i,
                )
                for i in (0, 1)
            ]
        )
        sinks = [{}, {}]
        tasks = []
        for i in (0, 1):
            first_step = 0.5 * block_first[slot][:, sides[i]] + 0.5 * sink[i]
            second_step = 0.5 * block_second[slot][:, sides[i]] + 0.5 * sink[i] * sink[i]
            direction = (first_step / (jnp.sqrt(second_step) + EPS_ADAM)).astype(BF)
            tasks.append(fetch(routes[i], direction, sinks[i]))
        run(*tasks)
        rotated_list.append(jnp.concatenate([sink[0], sink[1]], axis=1))
        mixed = [
            mm(
                lefts[i], jnp.concatenate([sinks[i][place] for place in range(n_fsdp)], axis=0)
            ).astype(BF)
            for i in (0, 1)
        ]
        update = mm_t(jnp.concatenate(mixed, axis=1), right_basis)
        master = pick(blocks, 0, my_blocks[slot])
        weight_list.append(master - LEARN_RATE * (update + DECAY_WEIGHT * master))
    used = my_used[:, None, None]
    rotated = jnp.stack(rotated_list)
    first_step = BETA_DECAY * block_first + (1.0 - BETA_DECAY) * rotated
    second_step = BETA_DECAY * block_second + (1.0 - BETA_DECAY) * rotated * rotated
    small_first_new = BETA_DECAY * small_first + (1.0 - BETA_DECAY) * small_grads
    small_second_new = BETA_DECAY * small_second + (1.0 - BETA_DECAY) * small_grads * small_grads
    small_weights = small_params - SMALL_RATE * small_first_new / (
        jnp.sqrt(small_second_new) + EPS_ADAM
    )
    return (
        layer_out,
        frames_grad,
        owned_list.astype(F32),
        first_step * used,
        second_step * used,
        jnp.stack(weight_list) * used,
        small_grads,
        small_weights,
        small_first_new,
        small_second_new,
    )


def solution(mesh):
    n_dp, n_fsdp = mesh.shape["dp"], mesh.shape["fsdp"]
    finer = Mesh(mesh.devices.reshape(n_dp // 2, 2, n_fsdp), AXES)
    placed = (
        P(AXES, None, None),
        P(AXES, None),
        P(AXES, None, None),
        P(None, "fsdp", None),
        P(),
        P(),
        P(DP, "fsdp", None),
        P(DP, None, None),
        P(DP, "fsdp", None),
        P(DP, "fsdp", None),
        P(),
        P(),
    )
    return jax.shard_map(
        per_device,
        mesh=finer,
        in_specs=placed,
        out_specs=(
            P(AXES, None, None),
            P(AXES, None, None),
            P(DP, "fsdp", None),
            P(DP, "fsdp", None),
            P(DP, "fsdp", None),
            P(DP, "fsdp", None),
            P(),
            P(),
            P(),
            P(),
        ),
        check_vma=False,
    )
```

```python
import jax
import jax.numpy as jnp
from jax import lax
from jax.experimental import pallas as pl
from jax.experimental.pallas import tpu as pltpu
from jax.sharding import Mesh
from jax.sharding import PartitionSpec as P

D = 1024
HEADS = 8
FF = 4096
KERNEL = 5
LENGTH = 512
HEAD = 128

EPS_NORM = 1e-05
EPS_ADAM = 1e-08
LEARN_RATE = 0.02
SMALL_RATE = 0.3
DECAY_WEIGHT = 0.01
BETA_DECAY = 0.5
MASKED = -1000000000.0
DP = ("dpz", "core")
AXES = (*DP, "fsdp")
BF = jnp.bfloat16
F32 = jnp.float32


def bits_of(size):
    return [1 << k for k in range(size.bit_length() - 1)]


def swap(value, dp_mask, fsdp_mask):
    n_dp, n_fsdp = lax.axis_size(DP), lax.axis_size("fsdp")
    pairs = [
        (d * n_fsdp + f, (d ^ dp_mask) * n_fsdp + (f ^ fsdp_mask))
        for d in range(n_dp)
        for f in range(n_fsdp)
    ]
    return lax.ppermute(value, AXES, pairs)


def swap_core(value):
    return swap(value, 1, 0)


def total(value):
    for mask in bits_of(lax.axis_size("fsdp")):
        value = value + swap(value, 0, mask)
    for mask in bits_of(lax.axis_size(DP)):
        value = value + swap(value, mask, 0)
    return value


class Route:
    def __init__(self, axis, flip):
        self.axis = axis
        if axis == "fsdp":
            self.size = lax.axis_size("fsdp")
            self.here = lax.axis_index("fsdp").astype(jnp.int32)
        else:
            self.size = lax.axis_size(DP) // 2
            self.here = lax.axis_index(DP).astype(jnp.int32) // 2
        self.bits = bits_of(self.size)
        if flip:
            self.bits = self.bits[::-1]
        self.differ = [0]
        for bit in self.bits[::-1]:
            self.differ = self.differ + [held | bit for held in self.differ]

    def trade(self, value, step):
        bit = self.bits[step]
        return swap(value, 0, bit) if self.axis == "fsdp" else swap(value, 2 * bit, 0)

    def indices(self):
        return self.here ^ jnp.array(self.differ, jnp.int32)


def after(value, *earlier):
    return lax.optimization_barrier((value, *earlier))[0]


def pick(value, axis, index):
    return lax.dynamic_index_in_dim(value, index, axis, keepdims=False)


def norm_apply(values, scale_row, shift_row):
    average = jnp.mean(values, axis=-1, keepdims=True)
    centered = values - average
    variance = jnp.mean(centered * centered, axis=-1, keepdims=True)
    return centered * lax.rsqrt(variance + EPS_NORM) * scale_row + shift_row


def swish(values):
    return values * jax.nn.sigmoid(values)


def depthwise(gated_rows, kernel_taps, segment_ids):
    length = gated_rows.shape[1]
    margin = KERNEL // 2
    padded = jnp.pad(gated_rows, ((0, 0), (margin, margin), (0, 0)))
    segment_pad = jnp.pad(segment_ids, ((0, 0), (margin, margin)), constant_values=-1)
    summed = jnp.zeros_like(gated_rows)
    for offset in range(KERNEL):
        matched = (segment_pad[:, offset : offset + length] == segment_ids)[:, :, None]
        summed = summed + kernel_taps[offset] * jnp.where(
            matched, padded[:, offset : offset + length], 0.0
        )
    return summed


def slot_tables(owners, groups, count_blocks):
    capacity = (count_blocks + groups - 1) // groups
    block_index = jnp.arange(count_blocks, dtype=jnp.int32)
    earlier = (owners[None, :] == owners[:, None]) & (block_index[None, :] < block_index[:, None])
    ranking = jnp.sum(earlier.astype(jnp.int32), axis=1)
    slot_of = owners * capacity + ranking
    return slot_of[None, :] == jnp.arange(capacity * groups, dtype=jnp.int32)[:, None]


def gated_conv(pre_a, pre_g, kernel_taps, segment_ids):
    rows_here = segment_ids.shape[0]
    gated_rows = pre_a * jax.nn.sigmoid(pre_g)
    shaped = gated_rows.reshape(rows_here, -1, gated_rows.shape[-1])
    return depthwise(shaped, kernel_taps, segment_ids).reshape(gated_rows.shape)


def masked_scores(queries, keys_row, segment_row):
    scores = jnp.einsum("qhe,khe->hqk", queries, keys_row, preferred_element_type=F32)
    matched = (segment_row[:, None] == segment_row[None, :])[None]
    return jnp.where(matched, scores, MASKED)


def attend_forward(arrays):
    queries, keys_row, values_row, segment_row = arrays
    scores = masked_scores(queries, keys_row, segment_row)
    highest = jnp.max(scores, axis=-1, keepdims=True)
    exponent = jnp.exp(scores - highest)
    summed = jnp.sum(exponent, axis=-1, keepdims=True)
    attention = (exponent / summed).astype(BF)
    context = jnp.einsum("hqk,khe->qhe", attention, values_row, preferred_element_type=F32)
    return (context, (highest + jnp.log(summed))[..., 0])


def attend_backward(arrays):
    queries, keys_row, values_row, segment_row, log_total, context_grad = arrays
    scores = masked_scores(queries, keys_row, segment_row)
    attention = jnp.exp(scores - log_total[..., None])
    attention_grad = jnp.einsum(
        "qhe,khe->hqk", context_grad, values_row, preferred_element_type=F32
    )
    score_grad = attention * (
        attention_grad - jnp.sum(attention_grad * attention, axis=-1, keepdims=True)
    )
    score_low = score_grad.astype(BF)
    query_grad = jnp.einsum("hqk,khe->qhe", score_low, keys_row, preferred_element_type=F32)
    key_grad = jnp.einsum("hqk,qhe->khe", score_low, queries, preferred_element_type=F32)
    value_grad = jnp.einsum(
        "hqk,qhe->khe", attention.astype(BF), context_grad, preferred_element_type=F32
    )
    return (query_grad, key_grad, value_grad)


def mm(left, right):
    return jnp.dot(left, right, preferred_element_type=F32)


def mm_t(left, right):
    return lax.dot_general(left, right, (((1,), (1,)), ((), ())), preferred_element_type=F32)


def t_mm(left, right):
    return lax.dot_general(left, right, (((0,), (0,)), ((), ())), preferred_element_type=F32)


def interleave(side, shard, fetched, arrived, local):
    count, n_shards, size, _ = fetched.shape

    def kernel(at_ref, fetched_ref, arrived_ref, local_ref, out_ref):
        near, here = at_ref[0], at_ref[1]
        for i in range(n_shards):
            at = pl.multiple_of((2 * i + near) * size, size)
            out_ref[0, pl.ds(at, size), :] = fetched_ref[0, i]
            at = pl.multiple_of((2 * (here ^ i) + 1 - near) * size, size)
            out_ref[0, pl.ds(at, size), :] = arrived_ref[0, i - 1] if i else local_ref[0]

    return pl.pallas_call(
        kernel,
        grid_spec=pltpu.PrefetchScalarGridSpec(
            num_scalar_prefetch=1,
            grid=(count,),
            in_specs=[
                pl.BlockSpec((1, n_shards, size, D), lambda b, s: (b, 0, 0, 0)),
                pl.BlockSpec((1, n_shards - 1, size, D), lambda b, s: (b, 0, 0, 0)),
                pl.BlockSpec((1, size, D), lambda b, s: (b, 0, 0)),
            ],
            out_specs=pl.BlockSpec((1, D, D), lambda b, s: (b, 0, 0)),
        ),
        out_shape=jax.ShapeDtypeStruct((count, D, D), BF),
        cost_estimate=pl.CostEstimate(
            flops=0, bytes_accessed=count * 4 * D * D, transcendentals=0
        ),
        name="interleave",
    )(jnp.stack([side, shard]), fetched, arrived, local)


def turn(starts, square):
    count = square.shape[0]
    n_shards = starts.shape[0]
    size = D // n_shards

    def kernel(starts_ref, square_ref, out_ref):
        for place in range(n_shards):
            at = pl.multiple_of(starts_ref[place] * size, size)
            out_ref[0, :, place * size : (place + 1) * size] = square_ref[0, :, pl.ds(at, size)]

    return pl.pallas_call(
        kernel,
        grid_spec=pltpu.PrefetchScalarGridSpec(
            num_scalar_prefetch=1,
            grid=(count, n_shards),
            in_specs=[pl.BlockSpec((1, size, D), lambda b, i, s: (b, s[i], 0))],
            out_specs=pl.BlockSpec((1, size, D), lambda b, i, s: (b, i, 0)),
        ),
        out_shape=jax.ShapeDtypeStruct(square.shape, square.dtype),
        cost_estimate=pl.CostEstimate(
            flops=0, bytes_accessed=count * 4 * D * D, transcendentals=0
        ),
        name="turn",
    )(starts, square)


def deal(chosen, used, parts):
    n_slots = chosen.shape[0]
    sizes = [part.shape[0] for part in parts]

    def kernel(chosen_ref, used_ref, *refs):
        *part_refs, out_ref, all_ref = refs
        at = 0
        for ref, size in zip(part_refs, sizes):
            all_ref[at : at + size] = ref[...]
            at += size
        for slot in range(n_slots):
            held = all_ref[chosen_ref[slot]].astype(F32)
            out_ref[slot] = (held * used_ref[slot].astype(F32)).astype(BF)

    return pl.pallas_call(
        kernel,
        in_specs=[pl.BlockSpec(memory_space=pltpu.SMEM)] * 2
        + [pl.BlockSpec(memory_space=pltpu.VMEM)] * len(parts),
        out_specs=pl.BlockSpec(memory_space=pltpu.VMEM),
        out_shape=jax.ShapeDtypeStruct((n_slots, *parts[0].shape[1:]), BF),
        scratch_shapes=[pltpu.VMEM((sum(sizes), *parts[0].shape[1:]), BF)],
        name="deal",
    )(chosen, used, *parts)


def regroup(starts, value, act=False, blocks=None):
    tokens = value.shape[0]
    blocks = list(range(value.shape[1] // D)) if blocks is None else blocks
    base, stride = blocks[0], (blocks[1] - blocks[0] if len(blocks) > 1 else 1)
    n_blocks = len(blocks)
    n_chunks = starts.shape[0]
    size = D // n_chunks
    if size % 128:
        value = jnp.concatenate([value[:, j * D : (j + 1) * D] for j in blocks], axis=1)
        value = swish(value.astype(F32)).astype(BF) if act else value
        split = value.reshape(tokens, n_blocks, n_chunks, size)
        return jnp.concatenate(
            [
                lax.dynamic_index_in_dim(split, starts[q], 2, keepdims=False).reshape(tokens, -1)
                for q in range(n_chunks)
            ],
            axis=1,
        )

    def kernel(starts_ref, value_ref, out_ref):
        block = pl.program_id(0)
        for place in range(n_chunks):
            at = pl.multiple_of(starts_ref[place] * size, size)
            held = value_ref[:, pl.ds(at, size)]
            if act:
                held = swish(held.astype(F32)).astype(BF)
            to = pl.multiple_of((place * n_blocks + block) * size, size)
            out_ref[:, pl.ds(to, size)] = held

    return pl.pallas_call(
        kernel,
        grid_spec=pltpu.PrefetchScalarGridSpec(
            num_scalar_prefetch=1,
            grid=(n_blocks,),
            in_specs=[pl.BlockSpec((tokens, D), lambda b, s: (0, base + stride * b))],
            out_specs=pl.BlockSpec((tokens, n_blocks * D), lambda b, s: (0, 0)),
        ),
        out_shape=jax.ShapeDtypeStruct((tokens, n_blocks * D), value.dtype),
        cost_estimate=pl.CostEstimate(
            flops=0, bytes_accessed=4 * tokens * n_blocks * D, transcendentals=0
        ),
        name="regroup",
    )(starts, value)


def run(*tasks):
    got = [None] * len(tasks)
    left = list(tasks)
    while left:
        going, wants = [], []
        for task, arrived in zip(left, got):
            try:
                wants.append(task.send(arrived))
                going.append(task)
            except StopIteration:
                pass
        left, got = going, wants


def fetch(route, own, sink):
    sink[0] = own
    for step in range(len(route.bits)):
        known = list(sink)
        got = yield [route.trade(sink[place], step) for place in known]
        for place, piece in zip(known, got):
            sink[place + (route.size >> (step + 1))] = piece


def low_add(left, right):
    return (left.astype(F32) + right.astype(F32)).astype(BF)


def halve(route, kept, sent, sink, name):
    for step in range(len(route.bits)):
        arrived = yield route.trade(sent, step)
        if step + 1 == len(route.bits):
            sink[name] = kept + arrived.astype(F32) if kept.dtype == F32 else low_add(kept, arrived)
            return
        part = kept.shape[0] // 2
        sent = low_add(kept[part:], arrived[part:])
        kept = kept[:part].astype(F32) + arrived[:part].astype(F32) if kept.dtype == F32 else low_add(
            kept[:part], arrived[:part]
        )


def halve_dp(route, held, sink, name):
    count, sides, rows, _ = held.shape
    piece = rows // route.size
    core = lax.axis_index(DP) % 2
    indices = route.indices()
    parts = [
        lax.dynamic_slice(held, (0, 0, indices[place] * piece, 0), (count, sides, piece, D))
        for place in range(route.size)
    ]
    middle = route.size // 2
    yield from halve(route, jnp.stack(parts[:middle]), jnp.stack(parts[middle:]), sink, name)
    held = sink[name][0]
    if sides == 1:
        sink[name] = held[:, 0]
        return
    arrived = yield swap_core(pick(held, 1, 1 - core))
    sink[name] = [pick(held, 1, core), arrived]


def both(value):
    return jnp.concatenate([value, swap_core(value)], axis=0)


def across(partial):
    tokens = partial.shape[0] // 2
    return partial[:tokens] + swap_core(partial[tokens:])


def per_device(
    frames,
    segment_ids,
    out_grad,
    blocks,
    small_params,
    owners,
    left_bases,
    right_bases,
    block_first,
    block_second,
    small_first,
    small_second,
):
    rows_here = frames.shape[0]
    tokens = rows_here * LENGTH
    n_blocks = blocks.shape[0]
    rows_own = blocks.shape[1]
    scale_head = HEAD ** (-0.5)
    n_dp = lax.axis_size(DP)
    n_fsdp = lax.axis_size("fsdp")
    mine = lax.axis_index("fsdp")
    count_all = tokens * n_dp * n_fsdp
    core = lax.axis_index("core").astype(jnp.int32)
    dpz = lax.axis_index("dpz").astype(jnp.int32)
    fsdp = lax.axis_index("fsdp").astype(jnp.int32)
    half = rows_own // 2
    per_in = FF // D
    per_core = per_in // 2
    base_attn = 2 * per_in
    base_last = base_attn + 7
    routes = [Route("fsdp", False), Route("fsdp", True)]
    routes_dp = [Route("dp", False), Route("dp", True)]
    shards = [route.indices() for route in routes]

    def rows_of(low, count, side, size):
        return lax.dynamic_slice(blocks, (low, side * size, 0), (count, size, D)).astype(BF)

    def own_share(base):
        own = [rows_of(base + k * per_in + core * per_core, per_core, 0, rows_own) for k in (0, 1)]
        return jnp.concatenate(own, axis=0)

    def fetch_own(own):
        fetched = lax.all_gather(own, "fsdp", axis=1, tiled=True)
        return [fetched[j] for j in range(2 * per_core)]

    def fetch_shared(base):
        side = dpz % 2
        listed = []
        for k in (0, 1):
            at = base + k * per_in + core * per_core
            listed.append([rows_of(at, per_core, held, half) for held in (side, 1 - side)])
        own = jnp.concatenate([held for held, _ in listed], axis=0)
        fetched = lax.all_gather(own, "fsdp", axis=1, tiled=True)
        fetched = fetched.reshape(2, per_core, n_fsdp, half, D)
        result = []
        for k in (0, 1):
            away = jnp.stack(
                [pick(fetched[k], 1, shard) for shard in [fsdp ^ i for i in range(1, n_fsdp)]], axis=1
            )
            arrived = swap(away, 2, 0)
            result.append(interleave(side, fsdp, fetched[k], arrived, listed[k][1]))
        return [held[j] for held in result for j in range(per_core)]

    def fetch_half(low, high):
        own = rows_of(low, high - low, core, half)
        return lax.all_gather(own, ("fsdp", "core"), axis=1, tiled=True)

    gains = small_params[0:5]
    shifts = small_params[5:10]
    bn_gain = small_params[10]
    bn_shift = small_params[11]
    kernel_taps = small_params[12 : 12 + KERNEL]

    def feed_up(hidden, index, weights):
        normed, pullback = jax.vjp(norm_apply, hidden, gains[index], shifts[index])
        pair = both(normed.astype(BF))
        return [mm(pair, weights[j]).astype(BF) for j in range(per_core)], pullback, pair

    def feed_down(hidden, lifted, weights):
        acted = [swish(up.astype(F32)).astype(BF) for up in lifted]
        result = across(sum(mm(acted[j], weights[per_core + j]) for j in range(per_core)))
        return hidden + 0.5 * result, acted

    def feed_back(gradient, lifted, acted, normed_pair, weights):
        pair = both((0.5 * gradient).astype(BF))
        lows, grads_in, grads_out = [], [], []
        for j in range(per_core):
            acted_grad = mm_t(pair, weights[per_core + j])
            up = lifted[j].astype(F32)
            gate = jax.nn.sigmoid(up)
            lows.append((acted_grad * (gate * (1.0 + up * (1.0 - gate)))).astype(BF))
        for j in range(per_core):
            grads_out.append(t_mm(acted[j], pair).astype(BF))
            grads_in.append(t_mm(normed_pair, lows[j]).astype(BF))
        listed = [held.reshape(n_fsdp, rows_own, D) for held in grads_in + grads_out]
        stacked = jnp.stack(listed, axis=1)
        lows, stacked = lax.optimization_barrier((lows, stacked))
        return across(sum(mm_t(lows[j], weights[j]) for j in range(per_core))), stacked

    last = []

    def scatter(stacked):
        if last:
            stacked = after(stacked, last[-1])
        summed = lax.psum_scatter(stacked, "fsdp", scatter_dimension=0, tiled=True)
        last.append(lax.optimization_barrier(summed))
        return last[-1][0]

    def share(products):
        split = [held.astype(BF).reshape(n_fsdp, 2, half, D) for held in products]
        arrived = swap_core(jnp.stack([pick(held, 1, 1 - core) for held in split], axis=1))
        kept = jnp.stack([pick(held, 1, core) for held in split], axis=1)
        return low_add(kept, arrived)

    def spread_dp(held, sides, name):
        middle = (held.shape[0] + 1) // 2
        tasks = []
        for route, part, place in zip(routes_dp, (held[:middle], held[middle:]), "xy"):
            shaped = part.reshape(part.shape[0], sides, half, D)
            tasks.append(halve_dp(route, shaped, sums, name + place))
        run(*tasks)

    sums = {}
    weights1 = fetch_shared(0)
    weights_middle = fetch_half(base_attn, base_last)
    start_x = frames.astype(F32).reshape(tokens, D)
    capacity = left_bases.shape[0]
    slots = range(capacity)
    near = fsdp ^ jnp.arange(n_fsdp, dtype=jnp.int32)
    rights = [regroup(near, right_bases[slot].astype(BF)) for slot in slots]
    firsts = [regroup(near, block_first[slot]) for slot in slots]
    seconds = [regroup(near, block_second[slot]) for slot in slots]
    start_x, own2, rights, firsts, seconds = lax.optimization_barrier(
        (start_x, own_share(base_last), rights, firsts, seconds)
    )
    weights2 = fetch_own(own2)
    w_attn, w_conv = weights_middle[:4], weights_middle[4:]
    lifted1, ffn1_pullback, normed_pair1 = feed_up(start_x, 0, weights1)
    first_x, acted1 = feed_down(start_x, lifted1, weights1)
    normed, attn_pullback = jax.vjp(norm_apply, first_x, gains[1], shifts[1])
    attn_low = normed.astype(BF)
    split_shape = (rows_here, LENGTH, HEADS, HEAD)
    queries = (mm(attn_low, w_attn[0]) * scale_head).astype(BF).reshape(split_shape)
    keys_all = mm(attn_low, w_attn[1]).astype(BF).reshape(split_shape)
    values_all = mm(attn_low, w_attn[2]).astype(BF).reshape(split_shape)
    context, log_total = lax.map(attend_forward, (queries, keys_all, values_all, segment_ids))
    context_low = context.reshape(tokens, D).astype(BF)
    second_x = first_x + mm(context_low, w_attn[3])
    normed, conv_pullback = jax.vjp(norm_apply, second_x, gains[2], shifts[2])
    conv_low = normed.astype(BF)
    convolved, gated_pullback = jax.vjp(
        lambda pre_a, pre_g, taps_in: gated_conv(pre_a, pre_g, taps_in, segment_ids),
        mm(conv_low, w_conv[0]),
        mm(conv_low, w_conv[1]),
        kernel_taps,
    )
    stats = jnp.stack([jnp.sum(convolved, axis=0), jnp.sum(convolved * convolved, axis=0)])
    stats = total(stats)
    average = stats[0] / count_all
    inverse_dev = lax.rsqrt(stats[1] / count_all - average * average + EPS_NORM)
    standard = (convolved - average) * inverse_dev
    activated, bn_swish_pullback = jax.vjp(swish, standard * bn_gain + bn_shift)
    activated_low = activated.astype(BF)
    third_x = second_x + mm(activated_low, w_conv[2])
    lifted2, ffn2_pullback, normed_pair2 = feed_up(third_x, 3, weights2)
    fourth_x, acted2 = feed_down(third_x, lifted2, weights2)
    layer_value, final_pullback = jax.vjp(norm_apply, fourth_x, gains[4], shifts[4])
    layer_out = layer_value.astype(BF).reshape(rows_here, LENGTH, D)

    grad_x, final_gain, final_shift = final_pullback(out_grad.astype(F32).reshape(tokens, D))
    normed_grad, stacked = feed_back(grad_x, lifted2, acted2, normed_pair2, weights2)
    hidden_grad, ffn2_gain, ffn2_shift = ffn2_pullback(normed_grad)
    grad_x = grad_x + hidden_grad
    branch_low = grad_x.astype(BF)
    (bn_grad,) = bn_swish_pullback(mm_t(branch_low, w_conv[2]))
    bn_sums = jnp.stack([jnp.sum(bn_grad, axis=0), jnp.sum(bn_grad * standard, axis=0)])
    bn_sums = total(bn_sums)
    summed2 = scatter(stacked)
    grad_back = t_mm(activated_low, branch_low)
    shift_sum, gain_sum = bn_sums[0], bn_sums[1]
    conv_grad = (
        bn_gain
        * inverse_dev
        * (bn_grad - shift_sum / count_all - standard * (gain_sum / count_all))
    )
    grad_a, grad_g, taps_grad = gated_pullback(conv_grad)
    grad_a, grad_g = grad_a.astype(BF), grad_g.astype(BF)
    shared_conv = share([t_mm(conv_low, grad_a), t_mm(conv_low, grad_g), grad_back])
    part_x, conv_gain, conv_shift = conv_pullback(
        mm_t(grad_a, w_conv[0]) + mm_t(grad_g, w_conv[1])
    )
    grad_x = grad_x + part_x
    branch_low = grad_x.astype(BF)
    context_grad = mm_t(branch_low, w_attn[3]).astype(BF).reshape(split_shape)
    query_grad, key_grad, value_grad = lax.map(
        attend_backward, (queries, keys_all, values_all, segment_ids, log_total, context_grad)
    )
    query_low = (query_grad.reshape(tokens, D) * scale_head).astype(BF)
    key_low = key_grad.reshape(tokens, D).astype(BF)
    value_low = value_grad.reshape(tokens, D).astype(BF)
    query_low, key_low, value_low, summed2, shared_conv = lax.optimization_barrier(
        (query_low, key_low, value_low, summed2, shared_conv)
    )
    summed_conv = scatter(shared_conv)
    grad_heads = [t_mm(attn_low, held) for held in (query_low, key_low, value_low)]
    grad_proj = t_mm(context_low, branch_low)
    part_x, attn_gain, attn_shift = attn_pullback(
        mm_t(query_low, w_attn[0]) + mm_t(key_low, w_attn[1]) + mm_t(value_low, w_attn[2])
    )
    grad_x = grad_x + part_x
    normed_grad, stacked = feed_back(grad_x, lifted1, acted1, normed_pair1, weights1)
    summed1 = scatter(stacked)
    spread_dp(summed2, 2, "ffn2")
    spread_dp(summed_conv, 1, "conv")
    summed_attn = scatter(
        after(
            share([*grad_heads, grad_proj]),
            *[sums[name + place] for name in ("ffn2", "conv") for place in "xy"],
        )
    )
    hidden_grad, ffn1_gain, ffn1_shift = ffn1_pullback(normed_grad)
    grad_x = grad_x + hidden_grad
    frames_grad = grad_x.reshape(rows_here, LENGTH, D)
    local_small = jnp.concatenate(
        [
            jnp.stack([ffn1_gain, attn_gain, conv_gain, ffn2_gain, final_gain]),
            jnp.stack([ffn1_shift, attn_shift, conv_shift, ffn2_shift, final_shift]),
            taps_grad,
        ],
        axis=0,
    )
    spread_dp(summed1, 2, "ffn1")
    summed_attn = after(summed_attn, *[sums["ffn1" + place] for place in "xy"])
    left_own = after(left_bases.astype(BF), summed_attn)
    left_all = lax.all_gather(left_own, "fsdp", axis=1, tiled=True)
    spread_dp(summed_attn, 1, "attn")
    summed_small = total(local_small)
    small_grads = jnp.concatenate(
        [summed_small[0:10], gain_sum[None], shift_sum[None], summed_small[10:]], axis=0
    )

    parts, places = [], []
    for name in ("ffn1", "middle", "ffn2"):
        base = sum(part.shape[0] for part in parts)
        if name == "middle":
            parts += [sums[name + place] for name in ("attn", "conv") for place in "xy"]
            places.append(base + jnp.arange(base_last - base_attn, dtype=jnp.int32))
            continue
        (in_mine, in_other), (out_mine, out_other) = sums[name + "x"], sums[name + "y"]
        parts += [in_mine, out_mine, in_other, out_other]
        index = jnp.arange(2 * per_in, dtype=jnp.int32)
        is_out, index = index // per_in, index % per_in
        away = (index // per_core != core).astype(jnp.int32)
        places.append(base + (2 * away + is_out) * per_core + index % per_core)
    places = jnp.concatenate(places)
    matches = slot_tables(owners, n_dp, n_blocks).astype(jnp.int32)
    slot_block = jnp.sum(matches * jnp.arange(n_blocks, dtype=jnp.int32)[None], axis=1)
    slot_used = jnp.sum(matches, axis=1)
    piece = half // (n_dp // 2)
    slot_place = jnp.sum(matches * places[None], axis=1)
    parts, frames_grad = lax.optimization_barrier((parts, frames_grad))
    sent = deal(slot_place, slot_used, parts).reshape(n_dp, capacity, piece, D)
    came = lax.all_to_all(sent, DP, 0, 0, tiled=False)
    came = came.reshape(n_dp // 2, 2, capacity, piece, D).transpose(2, 1, 0, 3, 4)
    owned_list = came.reshape(capacity, rows_own, D)

    dp_here = lax.axis_index(DP)
    my_blocks = lax.dynamic_slice_in_dim(slot_block, dp_here * capacity, capacity)
    my_used = lax.dynamic_slice_in_dim(slot_used, dp_here * capacity, capacity).astype(F32)
    lefts = turn(near, left_all)
    used = my_used[:, None, None]

    def exchange(value, axis):
        parts = jnp.split(value.astype(BF), n_fsdp, axis=axis)
        return [parts[0]] + [swap(parts[i], 0, i) for i in range(1, n_fsdp)]

    turned_list, weight_list = [], []
    for slot in slots:
        product = mm(owned_list[slot], rights[slot])
        columns = jnp.concatenate(exchange(product, 1), axis=0)
        turned = jnp.concatenate(exchange(t_mm(lefts[slot], columns), 0), axis=1)
        turned_list.append(turned)
        turned = turned.astype(F32)
        first_step = BETA_DECAY * firsts[slot] + (1.0 - BETA_DECAY) * turned
        second_step = BETA_DECAY * seconds[slot] + (1.0 - BETA_DECAY) * turned * turned
        direction = first_step / (jnp.sqrt(second_step) + EPS_ADAM)
        columns = jnp.concatenate(exchange(direction, 1), axis=0)
        mixed = jnp.concatenate(exchange(mm(lefts[slot], columns), 0), axis=1)
        update = mm_t(mixed, rights[slot])
        master = pick(blocks, 0, my_blocks[slot])
        weight_list.append(master - LEARN_RATE * (update + DECAY_WEIGHT * master))
    rotated = jnp.stack([regroup(near, turned) for turned in turned_list]).astype(F32)
    first_step = BETA_DECAY * block_first + (1.0 - BETA_DECAY) * rotated
    second_step = BETA_DECAY * block_second + (1.0 - BETA_DECAY) * rotated * rotated
    small_first_new = BETA_DECAY * small_first + (1.0 - BETA_DECAY) * small_grads
    small_second_new = BETA_DECAY * small_second + (1.0 - BETA_DECAY) * small_grads * small_grads
    small_weights = small_params - SMALL_RATE * small_first_new / (
        jnp.sqrt(small_second_new) + EPS_ADAM
    )
    return (
        layer_out,
        frames_grad,
        owned_list.astype(F32),
        first_step * used,
        second_step * used,
        jnp.stack(weight_list) * used,
        small_grads,
        small_weights,
        small_first_new,
        small_second_new,
    )


def solution(mesh):
    n_dp, n_fsdp = mesh.shape["dp"], mesh.shape["fsdp"]
    finer = Mesh(mesh.devices.reshape(n_dp // 2, 2, n_fsdp), AXES)
    placed = (
        P(AXES, None, None),
        P(AXES, None),
        P(AXES, None, None),
        P(None, "fsdp", None),
        P(),
        P(),
        P(DP, "fsdp", None),
        P(DP, None, None),
        P(DP, "fsdp", None),
        P(DP, "fsdp", None),
        P(),
        P(),
    )
    return jax.shard_map(
        per_device,
        mesh=finer,
        in_specs=placed,
        out_specs=(
            P(AXES, None, None),
            P(AXES, None, None),
            P(DP, "fsdp", None),
            P(DP, "fsdp", None),
            P(DP, "fsdp", None),
            P(DP, "fsdp", None),
            P(),
            P(),
            P(),
            P(),
        ),
        check_vma=False,
    )
```

```python
import jax
import jax.numpy as jnp
from jax import lax
from jax.experimental import pallas as pl
from jax.experimental.pallas import tpu as pltpu
from jax.sharding import Mesh
from jax.sharding import PartitionSpec as P

D = 1024
HEADS = 8
FF = 4096
KERNEL = 5
LENGTH = 512
HEAD = 128

EPS_NORM = 1e-05
EPS_ADAM = 1e-08
LEARN_RATE = 0.02
SMALL_RATE = 0.3
DECAY_WEIGHT = 0.01
BETA_DECAY = 0.5
MASKED = -1000000000.0
DP = ("dpz", "core")
AXES = (*DP, "fsdp")
BF = jnp.bfloat16
F32 = jnp.float32


def bits_of(size):
    return [1 << k for k in range(size.bit_length() - 1)]


def swap(value, dp_mask, fsdp_mask):
    n_dp, n_fsdp = lax.axis_size(DP), lax.axis_size("fsdp")
    pairs = [
        (d * n_fsdp + f, (d ^ dp_mask) * n_fsdp + (f ^ fsdp_mask))
        for d in range(n_dp)
        for f in range(n_fsdp)
    ]
    return lax.ppermute(value, AXES, pairs)


def swap_core(value):
    return swap(value, 1, 0)


def total(value):
    for mask in bits_of(lax.axis_size("fsdp")):
        value = value + swap(value, 0, mask)
    for mask in bits_of(lax.axis_size(DP)):
        value = value + swap(value, mask, 0)
    return value


class Route:
    def __init__(self, axis, flip):
        self.axis = axis
        if axis == "fsdp":
            self.size = lax.axis_size("fsdp")
            self.here = lax.axis_index("fsdp").astype(jnp.int32)
        else:
            self.size = lax.axis_size(DP) // 2
            self.here = lax.axis_index(DP).astype(jnp.int32) // 2
        self.bits = bits_of(self.size)
        if flip:
            self.bits = self.bits[::-1]
        self.differ = [0]
        for bit in self.bits[::-1]:
            self.differ = self.differ + [held | bit for held in self.differ]

    def trade(self, value, step):
        bit = self.bits[step]
        return swap(value, 0, bit) if self.axis == "fsdp" else swap(value, 2 * bit, 0)

    def indices(self):
        return self.here ^ jnp.array(self.differ, jnp.int32)


def after(value, *earlier):
    return lax.optimization_barrier((value, *earlier))[0]


def pick(value, axis, index):
    return lax.dynamic_index_in_dim(value, index, axis, keepdims=False)


def norm_apply(values, scale_row, shift_row):
    average = jnp.mean(values, axis=-1, keepdims=True)
    centered = values - average
    variance = jnp.mean(centered * centered, axis=-1, keepdims=True)
    return centered * lax.rsqrt(variance + EPS_NORM) * scale_row + shift_row


def swish(values):
    return values * jax.nn.sigmoid(values)


def depthwise(gated_rows, kernel_taps, segment_ids):
    length = gated_rows.shape[1]
    margin = KERNEL // 2
    padded = jnp.pad(gated_rows, ((0, 0), (margin, margin), (0, 0)))
    segment_pad = jnp.pad(segment_ids, ((0, 0), (margin, margin)), constant_values=-1)
    summed = jnp.zeros_like(gated_rows)
    for offset in range(KERNEL):
        matched = (segment_pad[:, offset : offset + length] == segment_ids)[:, :, None]
        summed = summed + kernel_taps[offset] * jnp.where(
            matched, padded[:, offset : offset + length], 0.0
        )
    return summed


def slot_tables(owners, groups, count_blocks):
    capacity = (count_blocks + groups - 1) // groups
    block_index = jnp.arange(count_blocks, dtype=jnp.int32)
    earlier = (owners[None, :] == owners[:, None]) & (block_index[None, :] < block_index[:, None])
    ranking = jnp.sum(earlier.astype(jnp.int32), axis=1)
    slot_of = owners * capacity + ranking
    return slot_of[None, :] == jnp.arange(capacity * groups, dtype=jnp.int32)[:, None]


def gated_conv(pre_a, pre_g, kernel_taps, segment_ids):
    rows_here = segment_ids.shape[0]
    gated_rows = pre_a * jax.nn.sigmoid(pre_g)
    shaped = gated_rows.reshape(rows_here, -1, gated_rows.shape[-1])
    return depthwise(shaped, kernel_taps, segment_ids).reshape(gated_rows.shape)


def masked_scores(queries, keys_row, segment_row):
    scores = jnp.einsum("qhe,khe->hqk", queries, keys_row, preferred_element_type=F32)
    matched = (segment_row[:, None] == segment_row[None, :])[None]
    return jnp.where(matched, scores, MASKED)


def attend_forward(arrays):
    queries, keys_row, values_row, segment_row = arrays
    scores = masked_scores(queries, keys_row, segment_row)
    highest = jnp.max(scores, axis=-1, keepdims=True)
    exponent = jnp.exp(scores - highest)
    summed = jnp.sum(exponent, axis=-1, keepdims=True)
    attention = (exponent / summed).astype(BF)
    context = jnp.einsum("hqk,khe->qhe", attention, values_row, preferred_element_type=F32)
    return (context, (highest + jnp.log(summed))[..., 0])


def attend_backward(arrays):
    queries, keys_row, values_row, segment_row, log_total, context_grad = arrays
    scores = masked_scores(queries, keys_row, segment_row)
    attention = jnp.exp(scores - log_total[..., None])
    attention_grad = jnp.einsum(
        "qhe,khe->hqk", context_grad, values_row, preferred_element_type=F32
    )
    score_grad = attention * (
        attention_grad - jnp.sum(attention_grad * attention, axis=-1, keepdims=True)
    )
    score_low = score_grad.astype(BF)
    query_grad = jnp.einsum("hqk,khe->qhe", score_low, keys_row, preferred_element_type=F32)
    key_grad = jnp.einsum("hqk,qhe->khe", score_low, queries, preferred_element_type=F32)
    value_grad = jnp.einsum(
        "hqk,qhe->khe", attention.astype(BF), context_grad, preferred_element_type=F32
    )
    return (query_grad, key_grad, value_grad)


def mm(left, right):
    return jnp.dot(left, right, preferred_element_type=F32)


def mm_t(left, right):
    return lax.dot_general(left, right, (((1,), (1,)), ((), ())), preferred_element_type=F32)


def t_mm(left, right):
    return lax.dot_general(left, right, (((0,), (0,)), ((), ())), preferred_element_type=F32)


def interleave(side, shard, fetched, arrived, local):
    count, n_shards, size, _ = fetched.shape

    def kernel(at_ref, fetched_ref, arrived_ref, local_ref, out_ref):
        near, here = at_ref[0], at_ref[1]
        for i in range(n_shards):
            at = pl.multiple_of((2 * i + near) * size, size)
            out_ref[0, pl.ds(at, size), :] = fetched_ref[0, i]
            at = pl.multiple_of((2 * (here ^ i) + 1 - near) * size, size)
            out_ref[0, pl.ds(at, size), :] = arrived_ref[0, i - 1] if i else local_ref[0]

    return pl.pallas_call(
        kernel,
        grid_spec=pltpu.PrefetchScalarGridSpec(
            num_scalar_prefetch=1,
            grid=(count,),
            in_specs=[
                pl.BlockSpec((1, n_shards, size, D), lambda b, s: (b, 0, 0, 0)),
                pl.BlockSpec((1, n_shards - 1, size, D), lambda b, s: (b, 0, 0, 0)),
                pl.BlockSpec((1, size, D), lambda b, s: (b, 0, 0)),
            ],
            out_specs=pl.BlockSpec((1, D, D), lambda b, s: (b, 0, 0)),
        ),
        out_shape=jax.ShapeDtypeStruct((count, D, D), BF),
        cost_estimate=pl.CostEstimate(
            flops=0, bytes_accessed=count * 4 * D * D, transcendentals=0
        ),
        name="interleave",
    )(jnp.stack([side, shard]), fetched, arrived, local)


def turn(starts, square):
    count = square.shape[0]
    n_shards = starts.shape[0]
    size = D // n_shards

    def kernel(starts_ref, square_ref, out_ref):
        for row in range(n_shards):
            rows = pl.ds(pl.multiple_of(starts_ref[row] * size, size), size)
            for column in range(n_shards):
                at = pl.multiple_of(starts_ref[column] * size, size)
                out_ref[0, row * size : (row + 1) * size, column * size : (column + 1) * size] = (
                    square_ref[0, rows, pl.ds(at, size)]
                )

    return pl.pallas_call(
        kernel,
        grid_spec=pltpu.PrefetchScalarGridSpec(
            num_scalar_prefetch=1,
            grid=(count,),
            in_specs=[pl.BlockSpec((1, D, D), lambda b, s: (b, 0, 0))],
            out_specs=pl.BlockSpec((1, D, D), lambda b, s: (b, 0, 0)),
        ),
        out_shape=jax.ShapeDtypeStruct(square.shape, square.dtype),
        compiler_params=pltpu.CompilerParams(vmem_limit_bytes=32 << 20),
        cost_estimate=pl.CostEstimate(
            flops=0, bytes_accessed=count * 4 * D * D, transcendentals=0
        ),
        name="turn",
    )(starts, square)


def deal(chosen, used, parts):
    n_slots = chosen.shape[0]
    sizes = [part.shape[0] for part in parts]

    def kernel(chosen_ref, used_ref, *refs):
        *part_refs, out_ref, all_ref = refs
        at = 0
        for ref, size in zip(part_refs, sizes):
            all_ref[at : at + size] = ref[...]
            at += size
        for slot in range(n_slots):
            held = all_ref[chosen_ref[slot]].astype(F32)
            out_ref[slot] = (held * used_ref[slot].astype(F32)).astype(BF)

    return pl.pallas_call(
        kernel,
        in_specs=[pl.BlockSpec(memory_space=pltpu.SMEM)] * 2
        + [pl.BlockSpec(memory_space=pltpu.VMEM)] * len(parts),
        out_specs=pl.BlockSpec(memory_space=pltpu.VMEM),
        out_shape=jax.ShapeDtypeStruct((n_slots, *parts[0].shape[1:]), BF),
        scratch_shapes=[pltpu.VMEM((sum(sizes), *parts[0].shape[1:]), BF)],
        name="deal",
    )(chosen, used, *parts)


def regroup(starts, value, act=False, blocks=None):
    tokens = value.shape[0]
    blocks = list(range(value.shape[1] // D)) if blocks is None else blocks
    base, stride = blocks[0], (blocks[1] - blocks[0] if len(blocks) > 1 else 1)
    n_blocks = len(blocks)
    n_chunks = starts.shape[0]
    size = D // n_chunks
    if size % 128:
        value = jnp.concatenate([value[:, j * D : (j + 1) * D] for j in blocks], axis=1)
        value = swish(value.astype(F32)).astype(BF) if act else value
        split = value.reshape(tokens, n_blocks, n_chunks, size)
        return jnp.concatenate(
            [
                lax.dynamic_index_in_dim(split, starts[q], 2, keepdims=False).reshape(tokens, -1)
                for q in range(n_chunks)
            ],
            axis=1,
        )

    def kernel(starts_ref, value_ref, out_ref):
        block = pl.program_id(0)
        for place in range(n_chunks):
            at = pl.multiple_of(starts_ref[place] * size, size)
            held = value_ref[:, pl.ds(at, size)]
            if act:
                held = swish(held.astype(F32)).astype(BF)
            to = pl.multiple_of((place * n_blocks + block) * size, size)
            out_ref[:, pl.ds(to, size)] = held

    return pl.pallas_call(
        kernel,
        grid_spec=pltpu.PrefetchScalarGridSpec(
            num_scalar_prefetch=1,
            grid=(n_blocks,),
            in_specs=[pl.BlockSpec((tokens, D), lambda b, s: (0, base + stride * b))],
            out_specs=pl.BlockSpec((tokens, n_blocks * D), lambda b, s: (0, 0)),
        ),
        out_shape=jax.ShapeDtypeStruct((tokens, n_blocks * D), value.dtype),
        cost_estimate=pl.CostEstimate(
            flops=0, bytes_accessed=4 * tokens * n_blocks * D, transcendentals=0
        ),
        name="regroup",
    )(starts, value)


def run(*tasks):
    got = [None] * len(tasks)
    left = list(tasks)
    while left:
        going, wants = [], []
        for task, arrived in zip(left, got):
            try:
                wants.append(task.send(arrived))
                going.append(task)
            except StopIteration:
                pass
        left, got = going, wants


def fetch(route, own, sink):
    sink[0] = own
    for step in range(len(route.bits)):
        known = list(sink)
        got = yield [route.trade(sink[place], step) for place in known]
        for place, piece in zip(known, got):
            sink[place + (route.size >> (step + 1))] = piece


def low_add(left, right):
    return (left.astype(F32) + right.astype(F32)).astype(BF)


def halve(route, kept, sent, sink, name):
    for step in range(len(route.bits)):
        arrived = yield route.trade(sent, step)
        if step + 1 == len(route.bits):
            sink[name] = kept + arrived.astype(F32) if kept.dtype == F32 else low_add(kept, arrived)
            return
        part = kept.shape[0] // 2
        sent = low_add(kept[part:], arrived[part:])
        kept = kept[:part].astype(F32) + arrived[:part].astype(F32) if kept.dtype == F32 else low_add(
            kept[:part], arrived[:part]
        )


def halve_dp(route, held, sink, name):
    count, sides, rows, _ = held.shape
    piece = rows // route.size
    core = lax.axis_index(DP) % 2
    indices = route.indices()
    parts = [
        lax.dynamic_slice(held, (0, 0, indices[place] * piece, 0), (count, sides, piece, D))
        for place in range(route.size)
    ]
    middle = route.size // 2
    yield from halve(route, jnp.stack(parts[:middle]), jnp.stack(parts[middle:]), sink, name)
    held = sink[name][0]
    if sides == 1:
        sink[name] = held[:, 0]
        return
    arrived = yield swap_core(pick(held, 1, 1 - core))
    sink[name] = [pick(held, 1, core), arrived]


def both(value):
    return jnp.concatenate([value, swap_core(value)], axis=0)


def across(partial):
    tokens = partial.shape[0] // 2
    return partial[:tokens] + swap_core(partial[tokens:])


def per_device(
    frames,
    segment_ids,
    out_grad,
    blocks,
    small_params,
    owners,
    left_bases,
    right_bases,
    block_first,
    block_second,
    small_first,
    small_second,
):
    rows_here = frames.shape[0]
    tokens = rows_here * LENGTH
    n_blocks = blocks.shape[0]
    rows_own = blocks.shape[1]
    scale_head = HEAD ** (-0.5)
    n_dp = lax.axis_size(DP)
    n_fsdp = lax.axis_size("fsdp")
    mine = lax.axis_index("fsdp")
    count_all = tokens * n_dp * n_fsdp
    core = lax.axis_index("core").astype(jnp.int32)
    dpz = lax.axis_index("dpz").astype(jnp.int32)
    fsdp = lax.axis_index("fsdp").astype(jnp.int32)
    half = rows_own // 2
    per_in = FF // D
    per_core = per_in // 2
    base_attn = 2 * per_in
    base_last = base_attn + 7
    routes = [Route("fsdp", False), Route("fsdp", True)]
    routes_dp = [Route("dp", False), Route("dp", True)]
    shards = [route.indices() for route in routes]

    def rows_of(low, count, side, size):
        return lax.dynamic_slice(blocks, (low, side * size, 0), (count, size, D)).astype(BF)

    def own_share(base):
        own = [rows_of(base + k * per_in + core * per_core, per_core, 0, rows_own) for k in (0, 1)]
        return jnp.concatenate(own, axis=0)

    def fetch_own(own):
        fetched = lax.all_gather(own, "fsdp", axis=1, tiled=True)
        return [fetched[j] for j in range(2 * per_core)]

    def fetch_shared(base):
        side = dpz % 2
        listed = []
        for k in (0, 1):
            at = base + k * per_in + core * per_core
            listed.append([rows_of(at, per_core, held, half) for held in (side, 1 - side)])
        own = jnp.concatenate([held for held, _ in listed], axis=0)
        fetched = lax.all_gather(own, "fsdp", axis=1, tiled=True)
        fetched = fetched.reshape(2, per_core, n_fsdp, half, D)
        result = []
        for k in (0, 1):
            away = jnp.stack(
                [pick(fetched[k], 1, shard) for shard in [fsdp ^ i for i in range(1, n_fsdp)]], axis=1
            )
            arrived = swap(away, 2, 0)
            result.append(interleave(side, fsdp, fetched[k], arrived, listed[k][1]))
        return [held[j] for held in result for j in range(per_core)]

    def fetch_half(low, high):
        own = rows_of(low, high - low, core, half)
        return lax.all_gather(own, ("fsdp", "core"), axis=1, tiled=True)

    gains = small_params[0:5]
    shifts = small_params[5:10]
    bn_gain = small_params[10]
    bn_shift = small_params[11]
    kernel_taps = small_params[12 : 12 + KERNEL]

    def feed_up(hidden, index, weights):
        normed, pullback = jax.vjp(norm_apply, hidden, gains[index], shifts[index])
        pair = both(normed.astype(BF))
        return [mm(pair, weights[j]).astype(BF) for j in range(per_core)], pullback, pair

    def feed_down(hidden, lifted, weights):
        acted = [swish(up.astype(F32)).astype(BF) for up in lifted]
        result = across(sum(mm(acted[j], weights[per_core + j]) for j in range(per_core)))
        return hidden + 0.5 * result, acted

    def feed_back(gradient, lifted, acted, normed_pair, weights):
        pair = both((0.5 * gradient).astype(BF))
        lows, grads_in, grads_out = [], [], []
        for j in range(per_core):
            acted_grad = mm_t(pair, weights[per_core + j])
            up = lifted[j].astype(F32)
            gate = jax.nn.sigmoid(up)
            lows.append((acted_grad * (gate * (1.0 + up * (1.0 - gate)))).astype(BF))
        for j in range(per_core):
            grads_out.append(t_mm(acted[j], pair).astype(BF))
            grads_in.append(t_mm(normed_pair, lows[j]).astype(BF))
        listed = [held.reshape(n_fsdp, rows_own, D) for held in grads_in + grads_out]
        stacked = jnp.stack(listed, axis=1)
        lows, stacked = lax.optimization_barrier((lows, stacked))
        return across(sum(mm_t(lows[j], weights[j]) for j in range(per_core))), stacked

    last = []

    def scatter(stacked):
        if last:
            stacked = after(stacked, last[-1])
        summed = lax.psum_scatter(stacked, "fsdp", scatter_dimension=0, tiled=True)
        last.append(lax.optimization_barrier(summed))
        return last[-1][0]

    def share(products):
        split = [held.astype(BF).reshape(n_fsdp, 2, half, D) for held in products]
        arrived = swap_core(jnp.stack([pick(held, 1, 1 - core) for held in split], axis=1))
        kept = jnp.stack([pick(held, 1, core) for held in split], axis=1)
        return low_add(kept, arrived)

    def spread_dp(held, sides, name):
        middle = (held.shape[0] + 1) // 2
        tasks = []
        for route, part, place in zip(routes_dp, (held[:middle], held[middle:]), "xy"):
            shaped = part.reshape(part.shape[0], sides, half, D)
            tasks.append(halve_dp(route, shaped, sums, name + place))
        run(*tasks)

    sums = {}
    weights1 = fetch_shared(0)
    weights_middle = fetch_half(base_attn, base_last)
    start_x = frames.astype(F32).reshape(tokens, D)
    capacity = left_bases.shape[0]
    slots = range(capacity)
    near = fsdp ^ jnp.arange(n_fsdp, dtype=jnp.int32)
    rights = [regroup(near, right_bases[slot].astype(BF)) for slot in slots]
    firsts = [regroup(near, block_first[slot]) for slot in slots]
    seconds = [regroup(near, block_second[slot]) for slot in slots]
    start_x, own2, rights, firsts, seconds = lax.optimization_barrier(
        (start_x, own_share(base_last), rights, firsts, seconds)
    )
    weights2 = fetch_own(own2)
    w_attn, w_conv = weights_middle[:4], weights_middle[4:]
    lifted1, ffn1_pullback, normed_pair1 = feed_up(start_x, 0, weights1)
    first_x, acted1 = feed_down(start_x, lifted1, weights1)
    normed, attn_pullback = jax.vjp(norm_apply, first_x, gains[1], shifts[1])
    attn_low = normed.astype(BF)
    split_shape = (rows_here, LENGTH, HEADS, HEAD)
    queries = (mm(attn_low, w_attn[0]) * scale_head).astype(BF).reshape(split_shape)
    keys_all = mm(attn_low, w_attn[1]).astype(BF).reshape(split_shape)
    values_all = mm(attn_low, w_attn[2]).astype(BF).reshape(split_shape)
    context, log_total = lax.map(attend_forward, (queries, keys_all, values_all, segment_ids))
    context_low = context.reshape(tokens, D).astype(BF)
    second_x = first_x + mm(context_low, w_attn[3])
    normed, conv_pullback = jax.vjp(norm_apply, second_x, gains[2], shifts[2])
    conv_low = normed.astype(BF)
    convolved, gated_pullback = jax.vjp(
        lambda pre_a, pre_g, taps_in: gated_conv(pre_a, pre_g, taps_in, segment_ids),
        mm(conv_low, w_conv[0]),
        mm(conv_low, w_conv[1]),
        kernel_taps,
    )
    stats = jnp.stack([jnp.sum(convolved, axis=0), jnp.sum(convolved * convolved, axis=0)])
    stats = total(stats)
    average = stats[0] / count_all
    inverse_dev = lax.rsqrt(stats[1] / count_all - average * average + EPS_NORM)
    standard = (convolved - average) * inverse_dev
    activated, bn_swish_pullback = jax.vjp(swish, standard * bn_gain + bn_shift)
    activated_low = activated.astype(BF)
    third_x = second_x + mm(activated_low, w_conv[2])
    lifted2, ffn2_pullback, normed_pair2 = feed_up(third_x, 3, weights2)
    fourth_x, acted2 = feed_down(third_x, lifted2, weights2)
    layer_value, final_pullback = jax.vjp(norm_apply, fourth_x, gains[4], shifts[4])
    layer_out = layer_value.astype(BF).reshape(rows_here, LENGTH, D)

    grad_x, final_gain, final_shift = final_pullback(out_grad.astype(F32).reshape(tokens, D))
    normed_grad, stacked = feed_back(grad_x, lifted2, acted2, normed_pair2, weights2)
    hidden_grad, ffn2_gain, ffn2_shift = ffn2_pullback(normed_grad)
    grad_x = grad_x + hidden_grad
    branch_low = grad_x.astype(BF)
    (bn_grad,) = bn_swish_pullback(mm_t(branch_low, w_conv[2]))
    bn_sums = jnp.stack([jnp.sum(bn_grad, axis=0), jnp.sum(bn_grad * standard, axis=0)])
    bn_sums = total(bn_sums)
    summed2 = scatter(stacked)
    grad_back = t_mm(activated_low, branch_low)
    shift_sum, gain_sum = bn_sums[0], bn_sums[1]
    conv_grad = (
        bn_gain
        * inverse_dev
        * (bn_grad - shift_sum / count_all - standard * (gain_sum / count_all))
    )
    grad_a, grad_g, taps_grad = gated_pullback(conv_grad)
    grad_a, grad_g = grad_a.astype(BF), grad_g.astype(BF)
    shared_conv = share([t_mm(conv_low, grad_a), t_mm(conv_low, grad_g), grad_back])
    part_x, conv_gain, conv_shift = conv_pullback(
        mm_t(grad_a, w_conv[0]) + mm_t(grad_g, w_conv[1])
    )
    grad_x = grad_x + part_x
    branch_low = grad_x.astype(BF)
    context_grad = mm_t(branch_low, w_attn[3]).astype(BF).reshape(split_shape)
    query_grad, key_grad, value_grad = lax.map(
        attend_backward, (queries, keys_all, values_all, segment_ids, log_total, context_grad)
    )
    query_low = (query_grad.reshape(tokens, D) * scale_head).astype(BF)
    key_low = key_grad.reshape(tokens, D).astype(BF)
    value_low = value_grad.reshape(tokens, D).astype(BF)
    query_low, key_low, value_low, summed2, shared_conv = lax.optimization_barrier(
        (query_low, key_low, value_low, summed2, shared_conv)
    )
    summed_conv = scatter(shared_conv)
    grad_heads = [t_mm(attn_low, held) for held in (query_low, key_low, value_low)]
    grad_proj = t_mm(context_low, branch_low)
    part_x, attn_gain, attn_shift = attn_pullback(
        mm_t(query_low, w_attn[0]) + mm_t(key_low, w_attn[1]) + mm_t(value_low, w_attn[2])
    )
    grad_x = grad_x + part_x
    normed_grad, stacked = feed_back(grad_x, lifted1, acted1, normed_pair1, weights1)
    summed1 = scatter(stacked)
    spread_dp(summed2, 2, "ffn2")
    spread_dp(summed_conv, 1, "conv")
    summed_attn = scatter(
        after(
            share([*grad_heads, grad_proj]),
            *[sums[name + place] for name in ("ffn2", "conv") for place in "xy"],
        )
    )
    hidden_grad, ffn1_gain, ffn1_shift = ffn1_pullback(normed_grad)
    grad_x = grad_x + hidden_grad
    frames_grad = grad_x.reshape(rows_here, LENGTH, D)
    local_small = jnp.concatenate(
        [
            jnp.stack([ffn1_gain, attn_gain, conv_gain, ffn2_gain, final_gain]),
            jnp.stack([ffn1_shift, attn_shift, conv_shift, ffn2_shift, final_shift]),
            taps_grad,
        ],
        axis=0,
    )
    spread_dp(summed1, 2, "ffn1")
    summed_attn = after(summed_attn, *[sums["ffn1" + place] for place in "xy"])
    left_own = after(left_bases.astype(BF), summed_attn)
    left_all = lax.all_gather(left_own, "fsdp", axis=1, tiled=True)
    spread_dp(summed_attn, 1, "attn")
    summed_small = total(local_small)
    small_grads = jnp.concatenate(
        [summed_small[0:10], gain_sum[None], shift_sum[None], summed_small[10:]], axis=0
    )

    parts, places = [], []
    for name in ("ffn1", "middle", "ffn2"):
        base = sum(part.shape[0] for part in parts)
        if name == "middle":
            parts += [sums[name + place] for name in ("attn", "conv") for place in "xy"]
            places.append(base + jnp.arange(base_last - base_attn, dtype=jnp.int32))
            continue
        (in_mine, in_other), (out_mine, out_other) = sums[name + "x"], sums[name + "y"]
        parts += [in_mine, out_mine, in_other, out_other]
        index = jnp.arange(2 * per_in, dtype=jnp.int32)
        is_out, index = index // per_in, index % per_in
        away = (index // per_core != core).astype(jnp.int32)
        places.append(base + (2 * away + is_out) * per_core + index % per_core)
    places = jnp.concatenate(places)
    matches = slot_tables(owners, n_dp, n_blocks).astype(jnp.int32)
    slot_block = jnp.sum(matches * jnp.arange(n_blocks, dtype=jnp.int32)[None], axis=1)
    slot_used = jnp.sum(matches, axis=1)
    piece = half // (n_dp // 2)
    slot_place = jnp.sum(matches * places[None], axis=1)
    parts, frames_grad = lax.optimization_barrier((parts, frames_grad))
    sent = deal(slot_place, slot_used, parts).reshape(n_dp, capacity, piece, D)
    came = lax.all_to_all(sent, DP, 0, 0, tiled=False)
    came = came.reshape(n_dp // 2, 2, capacity, piece, D).transpose(2, 1, 0, 3, 4)
    owned_list = came.reshape(capacity, rows_own, D)

    dp_here = lax.axis_index(DP)
    my_blocks = lax.dynamic_slice_in_dim(slot_block, dp_here * capacity, capacity)
    my_used = lax.dynamic_slice_in_dim(slot_used, dp_here * capacity, capacity).astype(F32)
    lefts = turn(near, left_all)
    used = my_used[:, None, None]

    def exchange(value, axis):
        parts = jnp.split(value.astype(BF), n_fsdp, axis=axis)
        return [parts[0]] + [swap(parts[i], 0, i) for i in range(1, n_fsdp)]

    turned_list, weight_list = [], []
    for slot in slots:
        product = mm(owned_list[slot], rights[slot])
        columns = jnp.concatenate(exchange(product, 1), axis=0)
        turned = jnp.concatenate(exchange(t_mm(lefts[slot], columns), 0), axis=1)
        turned_list.append(turned)
        turned = turned.astype(F32)
        first_step = BETA_DECAY * firsts[slot] + (1.0 - BETA_DECAY) * turned
        second_step = BETA_DECAY * seconds[slot] + (1.0 - BETA_DECAY) * turned * turned
        direction = first_step / (jnp.sqrt(second_step) + EPS_ADAM)
        columns = jnp.concatenate(exchange(direction, 1), axis=0)
        mixed = jnp.concatenate(exchange(mm(lefts[slot], columns), 0), axis=1)
        update = mm_t(mixed, rights[slot])
        master = pick(blocks, 0, my_blocks[slot])
        weight_list.append(master - LEARN_RATE * (update + DECAY_WEIGHT * master))
    rotated = regroup(near, jnp.concatenate(turned_list, axis=0)).astype(F32)
    rotated = rotated.reshape(capacity, rows_own, D)
    first_step = BETA_DECAY * block_first + (1.0 - BETA_DECAY) * rotated
    second_step = BETA_DECAY * block_second + (1.0 - BETA_DECAY) * rotated * rotated
    small_first_new = BETA_DECAY * small_first + (1.0 - BETA_DECAY) * small_grads
    small_second_new = BETA_DECAY * small_second + (1.0 - BETA_DECAY) * small_grads * small_grads
    small_weights = small_params - SMALL_RATE * small_first_new / (
        jnp.sqrt(small_second_new) + EPS_ADAM
    )
    return (
        layer_out,
        frames_grad,
        owned_list.astype(F32),
        first_step * used,
        second_step * used,
        jnp.stack(weight_list) * used,
        small_grads,
        small_weights,
        small_first_new,
        small_second_new,
    )


def solution(mesh):
    n_dp, n_fsdp = mesh.shape["dp"], mesh.shape["fsdp"]
    finer = Mesh(mesh.devices.reshape(n_dp // 2, 2, n_fsdp), AXES)
    placed = (
        P(AXES, None, None),
        P(AXES, None),
        P(AXES, None, None),
        P(None, "fsdp", None),
        P(),
        P(),
        P(DP, "fsdp", None),
        P(DP, None, None),
        P(DP, "fsdp", None),
        P(DP, "fsdp", None),
        P(),
        P(),
    )
    return jax.shard_map(
        per_device,
        mesh=finer,
        in_specs=placed,
        out_specs=(
            P(AXES, None, None),
            P(AXES, None, None),
            P(DP, "fsdp", None),
            P(DP, "fsdp", None),
            P(DP, "fsdp", None),
            P(DP, "fsdp", None),
            P(),
            P(),
            P(),
            P(),
        ),
        check_vma=False,
    )
```
